32 devices in a mesh: seq: 4 (over y, core), wt: 8 (over z, x).
Axes of the slice: x: 2, y: 2, z: 4, core: 2. Of those that a mesh axis runs over, the one named last changes fastest.
Arguments:
- activations: bfloat16 [16, 512, 768], P('wt', 'seq'), may hold values from -6 to 6
- upstream: bfloat16 [16, 512, 768], P('wt', 'seq'), may hold values from -6 to 6
- first_scale: bfloat16 [2, 768], P(None, 'wt'), may hold values from 0.5 to 1.5
- first_shift: bfloat16 [2, 768], P(None, 'wt'), may hold values from -1 to 1
- query_weight: bfloat16 [2, 768, 768], P(None, 'wt'), may hold values from -0.21875 to 0.21875
- query_bias: bfloat16 [2, 768], P(None, 'wt'), may hold values from -1 to 1
- key_weight: bfloat16 [2, 768, 768], P(None, 'wt'), may hold values from -0.21875 to 0.21875
- value_weight: bfloat16 [2, 768, 768], P(None, 'wt'), may hold values from -0.21875 to 0.21875
- value_bias: bfloat16 [2, 768], P(None, 'wt'), may hold values from -1 to 1
- output_weight: bfloat16 [2, 768, 768], P(None, 'wt'), may hold values from -0.75 to 0.75
- output_bias: bfloat16 [2, 768], P(None, 'wt'), may hold values from -1 to 1
- second_scale: bfloat16 [2, 768], P(None, 'wt'), may hold values from 0.5 to 1.5
- second_shift: bfloat16 [2, 768], P(None, 'wt'), may hold values from -1 to 1
- up_weight: bfloat16 [2, 768, 3072], P(None, 'wt'), may hold values from -0.21875 to 0.21875
- up_bias: bfloat16 [2, 3072], P(None, 'wt'), may hold values from -1 to 1
- down_weight: bfloat16 [2, 3072, 768], P(None, 'wt'), may hold values from -0.109375 to 0.109375
- down_bias: bfloat16 [2, 768], P(None, 'wt'), may hold values from -1 to 1
Outputs:
- result: bfloat16 [16, 512, 768], P('wt', 'seq')
- input_grad: float32 [16, 512, 768], P('wt', 'seq')
- first_scale_grad: float32 [2, 768], P(None, 'wt')
- first_shift_grad: float32 [2, 768], P(None, 'wt')
- query_weight_grad: float32 [2, 768, 768], P(None, 'wt')
- query_bias_grad: float32 [2, 768], P(None, 'wt')
- key_weight_grad: float32 [2, 768, 768], P(None, 'wt')
- value_weight_grad: float32 [2, 768, 768], P(None, 'wt')
- value_bias_grad: float32 [2, 768], P(None, 'wt')
- output_weight_grad: float32 [2, 768, 768], P(None, 'wt')
- output_bias_grad: float32 [2, 768], P(None, 'wt')
- second_scale_grad: float32 [2, 768], P(None, 'wt')
- second_shift_grad: float32 [2, 768], P(None, 'wt')
- up_weight_grad: float32 [2, 768, 3072], P(None, 'wt')
- up_bias_grad: float32 [2, 3072], P(None, 'wt')
- down_weight_grad: float32 [2, 3072, 768], P(None, 'wt')
- down_bias_grad: float32 [2, 768], P(None, 'wt')
The draws below stay inside these ranges and needn't reach their ends.
All inputs are finite; a program needn't handle non-finite values.
Results may differ from the reference program's by a relative error of at most 0.015.
Values may be sent and summed in bfloat16 or wider, within the bound.
No kernel may reach another device: no remote copies, remote signals or barrier semaphores. Data moves between devices by JAX's collectives and lax.ppermute only.
A program may use at most 256 MiB of HBM per device.

```python
import math
import jax
import jax.numpy as jnp
from jax import lax

D = 768
HEADS = 12
HEAD_DIM = 64
FF = 3072
FRAMES = 512
LAYERS = 2
CLIPS = 16


def block_scale(stream_key, dims, cuts, least, top_value):
    def one(position, shards_of):
        heights = jax.random.uniform(jax.random.fold_in(jax.random.fold_in(stream_key, 6), position), (shards_of,), jnp.float32, least / len(cuts), top_value / len(cuts))
        return jnp.repeat(jnp.exp(heights), dims[position] // shards_of).reshape((-1,) + (1,) * (len(dims) - position - 1))

    loudness = one(*cuts[0])
    for cut in cuts[1:]:
        loudness = loudness * one(*cut)
    return loudness


def gaussian(own_key, extent, width, reach, cuts=(), held_as=jnp.bfloat16):
    array = jax.random.normal(own_key, extent, jnp.float32) * width
    if len(cuts) > 0:
        array = block_scale(own_key, extent, cuts, -0.22, 0.18) * array
    return jnp.clip(array, min=-reach, max=reach).astype(held_as)


def setup_inputs(seed: int = 0) -> dict:
    arg_keys = jax.random.split(jax.random.key(seed), 18)
    activations = gaussian(arg_keys[0], (CLIPS, FRAMES, D), 1.0, 6.0, ((0, 8), (1, 4)))
    upstream = gaussian(arg_keys[1], (CLIPS, FRAMES, D), 1.0, 6.0, ((0, 8), (1, 4)))
    first_scale = jnp.clip(1.0 + 0.1 * jax.random.normal(arg_keys[2], (LAYERS, D), jnp.float32), 0.5, 1.5).astype(jnp.bfloat16)
    first_shift = gaussian(arg_keys[3], (LAYERS, D), 0.2, 1.0, ((1, 8),))
    query_weight = gaussian(arg_keys[4], (LAYERS, D, D), D ** -0.5, 0.21875, ((1, 8),))
    query_bias = gaussian(arg_keys[5], (LAYERS, D), 0.2, 1.0, ((1, 8),))
    key_weight = gaussian(arg_keys[6], (LAYERS, D, D), D ** -0.5, 0.21875, ((1, 8),))
    value_weight = gaussian(arg_keys[7], (LAYERS, D, D), D ** -0.5, 0.21875, ((1, 8),))
    value_bias = gaussian(arg_keys[8], (LAYERS, D), 0.2, 1.0, ((1, 8),))
    output_weight = gaussian(arg_keys[9], (LAYERS, D, D), HEAD_DIM ** -0.5, 0.75, ((1, 8),))
    output_bias = gaussian(arg_keys[10], (LAYERS, D), 0.2, 1.0, ((1, 8),))
    second_scale = jnp.clip(1.0 + 0.1 * jax.random.normal(arg_keys[11], (LAYERS, D), jnp.float32), 0.5, 1.5).astype(jnp.bfloat16)
    second_shift = gaussian(arg_keys[12], (LAYERS, D), 0.2, 1.0, ((1, 8),))
    up_weight = gaussian(arg_keys[13], (LAYERS, D, FF), D ** -0.5, 0.21875, ((1, 8),))
    up_bias = gaussian(arg_keys[14], (LAYERS, FF), 0.2, 1.0, ((1, 8),))
    down_weight = gaussian(arg_keys[15], (LAYERS, FF, D), FF ** -0.5, 0.109375, ((1, 8),))
    down_bias = gaussian(arg_keys[16], (LAYERS, D), 0.2, 1.0, ((1, 8),))
    return dict(activations=activations, upstream=upstream, first_scale=first_scale, first_shift=first_shift, query_weight=query_weight, query_bias=query_bias, key_weight=key_weight, value_weight=value_weight, value_bias=value_bias, output_weight=output_weight, output_bias=output_bias, second_scale=second_scale, second_shift=second_shift, up_weight=up_weight, up_bias=up_bias, down_weight=down_weight, down_bias=down_bias)


@jax.custom_vjp
def low(v):
    return lax.optimization_barrier(v.astype(jnp.bfloat16)).astype(jnp.float32)

@jax.custom_vjp
def low_back(v):
    return v

def low_keep(v):
    return (low(v), None)

def low_pass(kept, grad):
    return (grad,)

def back_keep(v):
    return (v, None)

def back_low(kept, grad):
    return (low(grad),)
low.defvjp(low_keep, low_pass)
low_back.defvjp(back_keep, back_low)
epsilon = 1e-05
highest = lax.Precision.HIGHEST

def layer_norm(values, scales, shifts):
    centred = values - lax.optimization_barrier(jnp.mean(values, axis=-1, keepdims=True))
    spread = lax.optimization_barrier(jnp.mean(centred * centred, axis=-1, keepdims=True))
    return centred * lax.rsqrt(spread + epsilon) * scales + shifts

def project(values, matrix):
    return jnp.dot(values, matrix, precision=highest, preferred_element_type=jnp.float32)

def attend_clip(triple):
    queries, keyset, valueset = triple
    factor = 1.0 / math.sqrt(HEAD_DIM)
    scores = low_back(jnp.einsum('qhd,khd->hqk', queries, keyset, precision=highest) * factor)
    chances = jax.nn.softmax(scores, axis=-1)
    return jnp.einsum('hqk,khd->qhd', low(chances), valueset, precision=highest)

def forward(inputs, parameters):
    bundle = inputs.shape[0]
    hidden = inputs
    heads_shape = (bundle, FRAMES, HEADS, HEAD_DIM)
    for layer_index in range(LAYERS):
        first_scale, first_shift, query_weight, query_bias, key_weight, value_weight, value_bias, output_weight, output_bias, second_scale, second_shift, up_weight, up_bias, down_weight, down_bias = tuple((member[layer_index] for member in parameters))
        normed = low(layer_norm(hidden, first_scale, first_shift))
        queries = low_back(low(project(normed, query_weight) + query_bias))
        keyset = low_back(low(project(normed, key_weight)))
        valueset = low_back(low(project(normed, value_weight) + value_bias))
        mixture = lax.map(jax.checkpoint(attend_clip), (queries.reshape(heads_shape), keyset.reshape(heads_shape), valueset.reshape(heads_shape)))
        mixture = low_back(low(mixture.reshape(bundle, FRAMES, D)))
        hidden = hidden + low_back(project(mixture, output_weight) + output_bias)
        second = low(layer_norm(hidden, second_scale, second_shift))
        upward = low_back(project(second, up_weight) + up_bias)
        activated = low(jax.nn.gelu(upward, approximate=False))
        hidden = hidden + low_back(project(activated, down_weight) + down_bias)
    return hidden

def reference(activations, upstream, first_scale, first_shift, query_weight, query_bias, key_weight, value_weight, value_bias, output_weight, output_bias, second_scale, second_shift, up_weight, up_bias, down_weight, down_bias):
    parameters = tuple((member.astype(jnp.float32) for member in (first_scale, first_shift, query_weight, query_bias, key_weight, value_weight, value_bias, output_weight, output_bias, second_scale, second_shift, up_weight, up_bias, down_weight, down_bias)))
    bundle = math.gcd(CLIPS, 8)
    bundles = CLIPS // bundle
    blocked_in = activations.reshape(bundles, bundle, FRAMES, D)
    blocked_up = upstream.reshape(bundles, bundle, FRAMES, D)

    def one_bundle(totals, pieces):
        block_in, block_up = pieces
        output, pullback = jax.vjp(forward, block_in.astype(jnp.float32), parameters)
        grad_in, grad_params = pullback(block_up.astype(jnp.float32))
        totals = tuple((first + second for first, second in zip(totals, grad_params)))
        return (totals, (output.astype(jnp.bfloat16), grad_in))
    starts = tuple((jnp.zeros_like(member) for member in parameters))
    totals, (outputs, grads_in) = lax.scan(one_bundle, starts, (blocked_in, blocked_up))
    return (outputs.reshape(CLIPS, FRAMES, D), grads_in.reshape(CLIPS, FRAMES, D), totals[0], totals[1], totals[2], totals[3], totals[4], totals[5], totals[6], totals[7], totals[8], totals[9], totals[10], totals[11], totals[12], totals[13], totals[14])
```

```python
import math

import jax
import jax.numpy as jnp
from jax import lax
from jax.experimental import pallas as pl
from jax.experimental.pallas import tpu as pltpu
from jax.sharding import PartitionSpec as P

HEAD_DIM = 64
LAYERS = 2
epsilon = 1e-05
BF = jnp.bfloat16
F32 = jnp.float32
VMEM_BYTES = 48 * 1024 * 1024

VECTORS = (
    "first_scale",
    "first_shift",
    "query_bias",
    "value_bias",
    "output_bias",
    "second_scale",
    "second_shift",
    "up_bias",
    "down_bias",
)


def matmul(left, right):
    return jnp.dot(left, right, preferred_element_type=F32)


def left_product(left, right):
    return lax.dot_general(left, right, (((0,), (0,)), ((), ())), preferred_element_type=F32)


def right_product(left, right):
    return lax.dot_general(left, right, (((1,), (1,)), ((), ())), preferred_element_type=F32)


def column_sums(values):
    return jnp.sum(values, axis=0, dtype=F32)


def swap_core(values):
    pairs = [(i, i ^ 1) for i in range(lax.axis_size("seq"))]
    return lax.ppermute(values, "seq", pairs)


def swap_row(values):
    pairs = [(i, i ^ 2) for i in range(lax.axis_size("seq"))]
    return lax.ppermute(values, "seq", pairs)


def by_core(core, mine, theirs, axis):
    return jnp.where(
        core == 0,
        jnp.concatenate([mine, theirs], axis),
        jnp.concatenate([theirs, mine], axis),
    )


def gather_owners(shard):
    return lax.all_gather(shard, "wt", axis=0, tiled=True)


def sum_to_owner(values):
    mine = lax.psum_scatter(values.astype(BF), "wt", scatter_dimension=0, tiled=True)
    return mine.astype(F32) + swap_row(mine).astype(F32)


def attend_kernel(q_ref, k_ref, v_ref, o_ref):
    factor = 1.0 / math.sqrt(HEAD_DIM)
    for head in range(q_ref.shape[1] // HEAD_DIM):
        part = slice(head * HEAD_DIM, (head + 1) * HEAD_DIM)
        scores = right_product(q_ref[:, part], k_ref[:, part]) * factor
        raised = jnp.exp(scores - jnp.max(scores, axis=1, keepdims=True))
        chances = raised * (1.0 / jnp.sum(raised, axis=1, keepdims=True))
        o_ref[:, part] = matmul(chances.astype(BF), v_ref[:, part]).astype(BF)


def attend(qkv):
    rows, width = qkv.shape
    width //= 3
    block = 2 * HEAD_DIM
    steps = width // block
    return pl.pallas_call(
        attend_kernel,
        grid=(steps,),
        in_specs=[
            pl.BlockSpec((rows, block), lambda i: (0, i)),
            pl.BlockSpec((rows, block), lambda i: (0, steps + i)),
            pl.BlockSpec((rows, block), lambda i: (0, 2 * steps + i)),
        ],
        out_specs=pl.BlockSpec((rows, block), lambda i: (0, i)),
        out_shape=jax.ShapeDtypeStruct((rows, width), BF),
        compiler_params=pltpu.CompilerParams(vmem_limit_bytes=VMEM_BYTES),
        cost_estimate=pl.CostEstimate(
            flops=4 * rows * rows * width,
            bytes_accessed=8 * rows * width,
            transcendentals=rows * rows * width // HEAD_DIM,
        ),
        name="attend",
    )(qkv, qkv, qkv)


def attend_back_kernel(q_ref, k_ref, v_ref, eo_ref, eq_ref, ek_ref, ev_ref):
    factor = 1.0 / math.sqrt(HEAD_DIM)
    for head in range(q_ref.shape[1] // HEAD_DIM):
        part = slice(head * HEAD_DIM, (head + 1) * HEAD_DIM)
        queries, keys, eo = q_ref[:, part], k_ref[:, part], eo_ref[:, part]
        scores = right_product(keys, queries) * factor
        raised = jnp.exp(scores - jnp.max(scores, axis=0, keepdims=True))
        chances = raised * (1.0 / jnp.sum(raised, axis=0, keepdims=True))
        ep = right_product(v_ref[:, part], eo)
        ev_ref[:, part] = matmul(chances.astype(BF), eo).astype(BF)
        inner = jnp.sum(ep * chances, axis=0, keepdims=True)
        es = (chances * (ep - inner)).astype(BF)
        ek_ref[:, part] = (matmul(es, queries) * factor).astype(BF)
        eq_ref[:, part] = (left_product(keys, es) * factor).T.astype(BF)


def attend_back(qkv, eo):
    rows, width = eo.shape
    block = 2 * HEAD_DIM
    steps = width // block
    return pl.pallas_call(
        attend_back_kernel,
        grid=(steps,),
        in_specs=[
            pl.BlockSpec((rows, block), lambda i: (0, i)),
            pl.BlockSpec((rows, block), lambda i: (0, steps + i)),
            pl.BlockSpec((rows, block), lambda i: (0, 2 * steps + i)),
            pl.BlockSpec((rows, block), lambda i: (0, i)),
        ],
        out_specs=[pl.BlockSpec((rows, block), lambda i: (0, i))] * 3,
        out_shape=[jax.ShapeDtypeStruct((rows, width), BF)] * 3,
        compiler_params=pltpu.CompilerParams(vmem_limit_bytes=VMEM_BYTES),
        cost_estimate=pl.CostEstimate(
            flops=10 * rows * rows * width,
            bytes_accessed=14 * rows * width,
            transcendentals=rows * rows * width // HEAD_DIM,
        ),
        name="attend_back",
    )(qkv, qkv, qkv, eo)


def norm_parts(values):
    centred = values - jnp.mean(values, axis=-1, keepdims=True)
    spread = jnp.mean(centred * centred, axis=-1, keepdims=True)
    rate = lax.rsqrt(spread + epsilon)
    return centred * rate, rate


def norm_back(values, scale, grad):
    flat, rate = norm_parts(values)
    inner = grad * scale
    mean_inner = jnp.mean(inner, axis=-1, keepdims=True)
    mean_cross = jnp.mean(inner * flat, axis=-1, keepdims=True)
    before = rate * (inner - mean_inner - flat * mean_cross)
    return before, column_sums(grad * flat), column_sums(grad)


def gelu_parts(values):
    below = 0.5 * (1.0 + lax.erf(values * math.sqrt(0.5)))
    density = jnp.exp(-0.5 * values * values) * (1.0 / math.sqrt(2.0 * math.pi))
    return values * below, below + values * density


def per_device(
    activations,
    upstream,
    first_scale,
    first_shift,
    query_weight,
    query_bias,
    key_weight,
    value_weight,
    value_bias,
    output_weight,
    output_bias,
    second_scale,
    second_shift,
    up_weight,
    up_bias,
    down_weight,
    down_bias,
):
    owners = lax.axis_size("wt")
    place = lax.axis_index("seq")
    core, side = place % 2, place // 2
    frames_here, features = activations.shape[1:]
    half = features // 2
    shard = features // owners
    units = up_weight.shape[2]
    unit_shard = units // owners
    unit_half = unit_shard // 2

    def to_chip(values):
        kept = lax.dynamic_index_in_dim(values, side, 0, keepdims=False)
        sent = lax.dynamic_index_in_dim(values, 1 - side, 0, keepdims=False)
        mine = jnp.concatenate([kept, swap_row(sent)], 0)
        return by_core(core, mine, swap_core(mine), 0)

    def from_chip(mine):
        kept, sent = mine[:frames_here], mine[frames_here:]
        other = swap_row(sent)
        return jnp.where(side == 0, jnp.stack([kept, other]), jnp.stack([other, kept]))

    def own_rows(values):
        return lax.dynamic_slice_in_dim(values, core * 2 * frames_here, 2 * frames_here, 0)

    def half_columns(values):
        return lax.dynamic_slice_in_dim(values, core * half, half, 1)

    members = dict(
        first_scale=first_scale,
        first_shift=first_shift,
        query_bias=query_bias,
        value_bias=value_bias,
        output_bias=output_bias,
        second_scale=second_scale,
        second_shift=second_shift,
        up_bias=up_bias,
        down_bias=down_bias,
    )
    packed = jnp.concatenate([members[name] for name in VECTORS], 1)
    spread = lax.all_gather(packed, "wt", axis=0, tiled=False)
    vectors = []
    for layer in range(LAYERS):
        found, start = {}, 0
        for name in VECTORS:
            size = members[name].shape[1]
            found[name] = spread[:, layer, start : start + size].reshape(-1).astype(F32)
            start += size
        vectors.append(found)

    def unit_part(bias):
        return lax.dynamic_index_in_dim(
            bias.reshape(owners, 2, unit_half), core, 1, keepdims=False
        ).reshape(-1)

    weights = []
    for layer in range(LAYERS):
        branch = gather_owners(
            jnp.concatenate(
                [
                    half_columns(query_weight[layer]),
                    half_columns(key_weight[layer]),
                    half_columns(value_weight[layer]),
                    half_columns(output_weight[layer]),
                ],
                1,
            )
        )
        up = gather_owners(
            lax.dynamic_index_in_dim(
                up_weight[layer].reshape(shard, owners, 2, unit_half), core, 2, keepdims=False
            ).reshape(shard, units // 2)
        )
        down = gather_owners(
            lax.dynamic_slice_in_dim(down_weight[layer], core * unit_half, unit_half, 0)
        )
        out_half = branch[:, 3 * half :]
        out = by_core(core, out_half, swap_core(out_half), 1)
        weights.append((branch[:, : 3 * half], out, up, down))

    hidden = to_chip(activations).astype(F32)
    kept = []
    for layer in range(LAYERS):
        vec = vectors[layer]
        in_weight, out_weight, up, down = weights[layer]
        flat, _ = norm_parts(hidden)
        normed = (flat * vec["first_scale"] + vec["first_shift"]).astype(BF)
        in_bias = jnp.concatenate(
            [
                lax.dynamic_slice_in_dim(vec["query_bias"], core * half, half, 0),
                jnp.zeros((half,), F32),
                lax.dynamic_slice_in_dim(vec["value_bias"], core * half, half, 0),
            ]
        )
        qkv = (matmul(normed, in_weight) + in_bias).astype(BF)
        mixture_half = attend(qkv)
        mixture = by_core(core, mixture_half, swap_core(mixture_half), 1)
        middle = hidden + matmul(mixture, out_weight) + vec["output_bias"]
        flat, _ = norm_parts(middle)
        second = (flat * vec["second_scale"] + vec["second_shift"]).astype(BF)
        upward = matmul(second, up) + unit_part(vec["up_bias"])
        activated, slope = gelu_parts(upward)
        activated = activated.astype(BF)
        slope = slope.astype(BF)
        kept.append((hidden, normed, qkv, mixture, middle, second, activated, slope))
        partial = matmul(activated, down)
        if layer + 1 < LAYERS:
            hidden = middle + vec["down_bias"] + (partial + swap_core(partial.astype(BF)))
        else:
            theirs = lax.dynamic_slice_in_dim(
                partial, (1 - core) * 2 * frames_here, 2 * frames_here, 0
            )
            total = own_rows(partial) + swap_core(theirs.astype(BF))
            result = from_chip((own_rows(middle) + vec["down_bias"] + total).astype(BF))

    grad_hidden = to_chip(upstream).astype(F32)
    settled = [None] * LAYERS
    for layer in reversed(range(LAYERS)):
        vec = vectors[layer]
        in_weight, out_weight, up, down = weights[layer]
        hidden, normed, qkv, mixture, middle, second, activated, slope = kept[layer]
        grads = {}
        down_in = grad_hidden.astype(BF)
        grad_down = sum_to_owner(left_product(activated, down_in))
        grads["down_bias"] = column_sums(down_in)
        grad_upward = (slope.astype(F32) * right_product(down_in, down)).astype(BF)
        grad_up = sum_to_owner(left_product(second, grad_upward))
        grad_up_bias = column_sums(grad_upward)
        partial = right_product(grad_upward, up)
        grad_second = partial + swap_core(partial.astype(BF))
        before, grads["second_scale"], grads["second_shift"] = norm_back(
            middle, vec["second_scale"], grad_second
        )
        grad_middle = grad_hidden + before
        branch_in = grad_middle.astype(BF)
        grads["output_bias"] = column_sums(branch_in)
        grad_out = left_product(mixture, half_columns(branch_in))
        out_rows = lax.dynamic_slice_in_dim(out_weight, core * half, half, 0)
        grad_mixture = right_product(branch_in, out_rows).astype(BF)
        grad_qkv = jnp.concatenate(attend_back(qkv, grad_mixture), 1)
        grad_in = left_product(normed, grad_qkv)
        grad_branch = sum_to_owner(jnp.concatenate([grad_in, grad_out], 1))
        grad_in_bias = column_sums(grad_qkv)
        partial = right_product(grad_qkv, in_weight)
        if layer > 0:
            grad_normed = partial + swap_core(partial.astype(BF))
            before, grads["first_scale"], grads["first_shift"] = norm_back(
                hidden, vec["first_scale"], grad_normed
            )
            grad_hidden = grad_middle + before
        else:
            theirs = lax.dynamic_slice_in_dim(
                partial, (1 - core) * 2 * frames_here, 2 * frames_here, 0
            )
            grad_normed = own_rows(partial) + swap_core(theirs.astype(BF))
            before, grads["first_scale"], grads["first_shift"] = norm_back(
                own_rows(hidden), vec["first_scale"], grad_normed
            )
            input_grad = from_chip(own_rows(grad_middle) + before)

        first = (core == 0).astype(F32)
        for name in ("down_bias", "second_scale", "second_shift", "output_bias"):
            grads[name] = grads[name] * first
        if layer > 0:
            grads["first_scale"] = grads["first_scale"] * first
            grads["first_shift"] = grads["first_shift"] * first
        blank = jnp.zeros((half,), F32)
        grads["query_bias"] = by_core(core, grad_in_bias[:half], blank, 0)
        grads["value_bias"] = by_core(core, grad_in_bias[2 * half :], blank, 0)
        unit_rows = grad_up_bias.reshape(owners, 1, unit_half)
        grads["up_bias"] = by_core(core, unit_rows, jnp.zeros_like(unit_rows), 1).reshape(-1)
        packed = jnp.concatenate([grads[name].reshape(owners, -1) for name in VECTORS], 1)
        packed = lax.psum_scatter(packed, "wt", scatter_dimension=0, tiled=False)
        packed = packed + swap_row(packed)
        packed = packed + swap_core(packed)
        done, start = {}, 0
        for name in VECTORS:
            size = members[name].shape[1]
            done[name] = packed[start : start + size]
            start += size

        def both(mine):
            mine = mine.astype(BF)
            other = swap_core(mine).astype(F32)
            mine = mine.astype(F32)
            return jnp.where(core == 0, mine, other), jnp.where(core == 0, other, mine)

        low, high = both(grad_branch)
        for position, name in enumerate(
            ("query_weight", "key_weight", "value_weight", "output_weight")
        ):
            part = slice(position * half, (position + 1) * half)
            done[name] = jnp.concatenate([low[:, part], high[:, part]], 1)
        low, high = both(grad_up)
        done["up_weight"] = jnp.stack(
            [low.reshape(shard, owners, unit_half), high.reshape(shard, owners, unit_half)], 2
        ).reshape(shard, units)
        low, high = both(grad_down)
        done["down_weight"] = jnp.concatenate([low, high], 0)
        settled[layer] = done

    names = (
        "first_scale",
        "first_shift",
        "query_weight",
        "query_bias",
        "key_weight",
        "value_weight",
        "value_bias",
        "output_weight",
        "output_bias",
        "second_scale",
        "second_shift",
        "up_weight",
        "up_bias",
        "down_weight",
        "down_bias",
    )
    final = tuple(
        jnp.stack([settled[layer][name] for layer in range(LAYERS)]) for name in names
    )
    return (result, input_grad) + final


def solution(mesh):
    rows, vector, matrix = P("wt", "seq", None), P(None, "wt"), P(None, "wt", None)
    parameters = (
        vector,
        vector,
        matrix,
        vector,
        matrix,
        matrix,
        vector,
        matrix,
        vector,
        vector,
        vector,
        matrix,
        vector,
        matrix,
        vector,
    )
    specs = (rows, rows) + parameters
    return jax.shard_map(
        per_device, mesh=mesh, in_specs=specs, out_specs=specs, check_vma=False
    )
```

```python
import math

import jax
import jax.numpy as jnp
from jax import lax
from jax.experimental import pallas as pl
from jax.experimental.pallas import tpu as pltpu
from jax.sharding import PartitionSpec as P

HEAD_DIM = 64
LAYERS = 2
epsilon = 1e-05
BF = jnp.bfloat16
F32 = jnp.float32
VMEM_BYTES = 48 * 1024 * 1024

GATHER_ORDER = (("wide", 0), ("branch", 0), ("wide", 1), ("branch", 1))

VECTORS = (
    "first_scale",
    "first_shift",
    "query_bias",
    "value_bias",
    "output_bias",
    "second_scale",
    "second_shift",
    "down_bias",
)
LINE_STEPS = (1, 2)


def matmul(left, right):
    return jnp.dot(left, right, preferred_element_type=F32)


def left_product(left, right):
    return lax.dot_general(left, right, (((0,), (0,)), ((), ())), preferred_element_type=F32)


def right_product(left, right):
    return lax.dot_general(left, right, (((1,), (1,)), ((), ())), preferred_element_type=F32)


def column_sums(values):
    return jnp.sum(values, axis=0, dtype=F32)


def swap_core(values):
    pairs = [(i, i ^ 1) for i in range(lax.axis_size("seq"))]
    return lax.ppermute(values, "seq", pairs)


def swap_row(values):
    pairs = [(i, i ^ 2) for i in range(lax.axis_size("seq"))]
    return lax.ppermute(values, "seq", pairs)


def by_core(core, mine, theirs, axis):
    return jnp.where(
        core == 0,
        jnp.concatenate([mine, theirs], axis),
        jnp.concatenate([theirs, mine], axis),
    )


def swap_pair(values):
    pairs = [(i, i ^ 1) for i in range(lax.axis_size("wt"))]
    return lax.ppermute(values, "wt", pairs)


def shift_line(values, step):
    owners = lax.axis_size("wt")
    pairs = [(i, (i + 2 * step) % owners) for i in range(owners)]
    return lax.ppermute(values, "wt", pairs)


def picked(values, index, axis):
    return lax.dynamic_index_in_dim(values, index, axis, keepdims=False)


def after(values, earlier):
    return lax.optimization_barrier((values, earlier))[0]


def swap_line(values, step):
    pairs = [(i, i ^ (2 * step)) for i in range(lax.axis_size("wt"))]
    return lax.ppermute(values, "wt", pairs)


def doubled(values, step):
    return jnp.concatenate([values, swap_line(values, step)], 0)


def place_kernel(fill, where_ref, *refs):
    fill(where_ref, *refs)


def place(fill, where, sources, spots, name):
    depth = sources[0][0].shape[0]
    rows = sources[0][0].shape[1]
    size = sum(math.prod(spot) for spot in spots) * depth

    def spot_index(spot):
        blank = (0,) * len(spot)
        return lambda k, w: (jnp.bitwise_xor(w[0], k),) + blank

    return pl.pallas_call(
        lambda *refs: place_kernel(fill, *refs),
        grid_spec=pltpu.PrefetchScalarGridSpec(
            num_scalar_prefetch=1,
            grid=(depth,),
            in_specs=[
                pl.BlockSpec((1, rows, width), lambda k, w, block=block: (k, 0, block))
                for _, width, block in sources
            ],
            out_specs=[pl.BlockSpec((1,) + spot, spot_index(spot)) for spot in spots],
        ),
        out_shape=[jax.ShapeDtypeStruct((depth,) + spot, BF) for spot in spots],
        compiler_params=pltpu.CompilerParams(vmem_limit_bytes=VMEM_BYTES),
        cost_estimate=pl.CostEstimate(flops=0, bytes_accessed=4 * size, transcendentals=0),
        name=name,
    )(where, *(array for array, _, _ in sources))


def fill_in(where_ref, near_ref, far_ref, target):
    target[0, where_ref[1]] = near_ref[0]
    target[0, 1 - where_ref[1]] = far_ref[0]


def fill_out(where_ref, near_ref, far_ref, near_there_ref, far_there_ref, target):
    width = near_ref.shape[-1]
    here = pl.ds(pl.multiple_of(where_ref[3] * width, 128), width)
    there = pl.ds(pl.multiple_of((1 - where_ref[3]) * width, 128), width)
    target[0, where_ref[1], :, here] = near_ref[0]
    target[0, 1 - where_ref[1], :, here] = far_ref[0]
    target[0, where_ref[1], :, there] = near_there_ref[0]
    target[0, 1 - where_ref[1], :, there] = far_there_ref[0]


def fill_wide(where_ref, near_ref, far_ref, near_there_ref, far_there_ref, up, down):
    rows = near_ref.shape[1] // 2
    features = down.shape[-1]
    for source, across, over in (
        (near_ref, where_ref[1], where_ref[2]),
        (far_ref, 1 - where_ref[1], where_ref[2]),
        (near_there_ref, where_ref[1], 1 - where_ref[2]),
        (far_there_ref, 1 - where_ref[1], 1 - where_ref[2]),
    ):
        up[0, across, over] = source[0, :rows]
        down[0, across, over, 0] = source[0, rows:, :features]
        down[0, across, over, 1] = source[0, rows:, features:]


def reduce_line(values, kind):
    owners = lax.axis_size("wt")
    depth = owners // 2
    own = lax.axis_index("wt")
    line, across = own // 2, own % 2
    paired = values.reshape((depth, 2) + values.shape[1:])
    theirs = swap_pair(picked(paired, 1 - across, 1))
    mine = (picked(paired, across, 1).astype(F32) + theirs.astype(F32)).astype(kind)
    arrived = [
        shift_line(picked(mine, lax.rem(line + step, depth), 0), step) for step in range(1, depth)
    ]
    total = picked(mine, line, 0).astype(F32)
    for other in arrived:
        total = total + other.astype(F32)
    return total


def reduce_owners(values, kind=BF):
    if lax.axis_size("wt") == 8:
        return reduce_line(values, kind)
    return lax.psum_scatter(values, "wt", scatter_dimension=0, tiled=False).astype(F32)


def attend_kernel(q_ref, k_ref, v_ref, o_ref):
    factor = 1.0 / math.sqrt(HEAD_DIM)
    for head in range(q_ref.shape[1] // HEAD_DIM):
        part = slice(head * HEAD_DIM, (head + 1) * HEAD_DIM)
        scores = right_product(q_ref[:, part], k_ref[:, part]) * factor
        raised = jnp.exp(scores - jnp.max(scores, axis=1, keepdims=True))
        chances = raised * (1.0 / jnp.sum(raised, axis=1, keepdims=True))
        o_ref[:, part] = matmul(chances.astype(BF), v_ref[:, part]).astype(BF)


def attend(qkv):
    rows, width = qkv.shape
    width //= 3
    block = 2 * HEAD_DIM
    steps = width // block
    return pl.pallas_call(
        attend_kernel,
        grid=(steps,),
        in_specs=[
            pl.BlockSpec((rows, block), lambda i: (0, i)),
            pl.BlockSpec((rows, block), lambda i: (0, steps + i)),
            pl.BlockSpec((rows, block), lambda i: (0, 2 * steps + i)),
        ],
        out_specs=pl.BlockSpec((rows, block), lambda i: (0, i)),
        out_shape=jax.ShapeDtypeStruct((rows, width), BF),
        compiler_params=pltpu.CompilerParams(vmem_limit_bytes=VMEM_BYTES),
        cost_estimate=pl.CostEstimate(
            flops=4 * rows * rows * width,
            bytes_accessed=8 * rows * width,
            transcendentals=rows * rows * width // HEAD_DIM,
        ),
        name="attend",
    )(qkv, qkv, qkv)


def attend_back_kernel(q_ref, k_ref, v_ref, eo_ref, eq_ref, ek_ref, ev_ref):
    factor = 1.0 / math.sqrt(HEAD_DIM)
    for head in range(q_ref.shape[1] // HEAD_DIM):
        part = slice(head * HEAD_DIM, (head + 1) * HEAD_DIM)
        queries, keys, eo = q_ref[:, part], k_ref[:, part], eo_ref[:, part]
        scores = right_product(keys, queries) * factor
        raised = jnp.exp(scores - jnp.max(scores, axis=0, keepdims=True))
        chances = raised * (1.0 / jnp.sum(raised, axis=0, keepdims=True))
        ep = right_product(v_ref[:, part], eo)
        ev_ref[:, part] = matmul(chances.astype(BF), eo).astype(BF)
        inner = jnp.sum(ep * chances, axis=0, keepdims=True)
        es = (chances * (ep - inner)).astype(BF)
        ek_ref[:, part] = (matmul(es, queries) * factor).astype(BF)
        eq_ref[:, part] = (left_product(keys, es) * factor).T.astype(BF)


def attend_back(qkv, eo):
    rows, width = eo.shape
    block = 2 * HEAD_DIM
    steps = width // block
    return pl.pallas_call(
        attend_back_kernel,
        grid=(steps,),
        in_specs=[
            pl.BlockSpec((rows, block), lambda i: (0, i)),
            pl.BlockSpec((rows, block), lambda i: (0, steps + i)),
            pl.BlockSpec((rows, block), lambda i: (0, 2 * steps + i)),
            pl.BlockSpec((rows, block), lambda i: (0, i)),
        ],
        out_specs=[pl.BlockSpec((rows, block), lambda i: (0, i))] * 3,
        out_shape=[jax.ShapeDtypeStruct((rows, width), BF)] * 3,
        compiler_params=pltpu.CompilerParams(vmem_limit_bytes=VMEM_BYTES),
        cost_estimate=pl.CostEstimate(
            flops=10 * rows * rows * width,
            bytes_accessed=14 * rows * width,
            transcendentals=rows * rows * width // HEAD_DIM,
        ),
        name="attend_back",
    )(qkv, qkv, qkv, eo)


def norm_parts(values):
    centred = values - jnp.mean(values, axis=-1, keepdims=True)
    spread = jnp.mean(centred * centred, axis=-1, keepdims=True)
    rate = lax.rsqrt(spread + epsilon)
    return centred * rate, rate


def norm_back(values, scale, grad):
    flat, rate = norm_parts(values)
    inner = grad * scale
    mean_inner = jnp.mean(inner, axis=-1, keepdims=True)
    mean_cross = jnp.mean(inner * flat, axis=-1, keepdims=True)
    before = rate * (inner - mean_inner - flat * mean_cross)
    return before, column_sums(grad * flat), column_sums(grad)


def gelu_parts(values):
    below = 0.5 * (1.0 + lax.erf(values * math.sqrt(0.5)))
    density = jnp.exp(-0.5 * values * values) * (1.0 / math.sqrt(2.0 * math.pi))
    return values * below, below + values * density


def per_device(
    activations,
    upstream,
    first_scale,
    first_shift,
    query_weight,
    query_bias,
    key_weight,
    value_weight,
    value_bias,
    output_weight,
    output_bias,
    second_scale,
    second_shift,
    up_weight,
    up_bias,
    down_weight,
    down_bias,
):
    owners = lax.axis_size("wt")
    seat = lax.axis_index("seq")
    core, side = seat % 2, seat // 2
    frames_here, features = activations.shape[1:]
    half = features // 2
    shard = features // owners
    units = up_weight.shape[2]
    unit_shard = units // owners
    unit_half = unit_shard // 2

    def to_chip(values):
        kept = lax.dynamic_index_in_dim(values, side, 0, keepdims=False)
        sent = lax.dynamic_index_in_dim(values, 1 - side, 0, keepdims=False)
        mine = jnp.concatenate([kept, swap_row(sent)], 0)
        return by_core(core, mine, swap_core(mine), 0)

    def from_chip(mine):
        kept, sent = mine[:frames_here], mine[frames_here:]
        other = swap_row(sent)
        return jnp.where(side == 0, jnp.stack([kept, other]), jnp.stack([other, kept]))

    def own_rows(values):
        return lax.dynamic_slice_in_dim(values, core * 2 * frames_here, 2 * frames_here, 0)

    def half_columns(values):
        return lax.dynamic_slice_in_dim(values, core * half, half, 1)

    direct = owners == 8
    own = lax.axis_index("wt")
    line, across = own // 2, own % 2
    where = jnp.stack([line, across, side, core]).astype(jnp.int32)
    members = dict(
        first_scale=first_scale,
        first_shift=first_shift,
        query_bias=query_bias,
        value_bias=value_bias,
        output_bias=output_bias,
        second_scale=second_scale,
        second_shift=second_shift,
        down_bias=down_bias,
    )
    narrow = len(VECTORS) * shard
    packed = jnp.concatenate([members[name] for name in VECTORS] + [up_bias], 1)
    if direct:
        reached = packed[None]
        for step in LINE_STEPS:
            reached = doubled(reached, step)
        other = swap_pair(reached)
        spread = jnp.stack([reached, other], 1)
        for bit in LINE_STEPS:
            turned = spread.reshape((owners // (4 * bit), 2, bit, 2) + packed.shape)
            spread = jnp.where((line & bit) == 0, turned, turned[:, ::-1]).reshape(spread.shape)
        spread = jnp.where(across == 0, spread, spread[:, ::-1]).reshape(
            (owners,) + packed.shape
        )
    else:
        spread = lax.all_gather(packed, "wt", axis=0, tiled=False)
    vector_rows = (
        spread[:, :, :narrow]
        .reshape(owners, LAYERS * len(VECTORS), shard)
        .swapaxes(0, 1)
        .reshape(LAYERS * len(VECTORS), features)
        .astype(F32)
    )
    vectors = [
        {
            name: vector_rows[layer * len(VECTORS) + position]
            for position, name in enumerate(VECTORS)
        }
        for layer in range(LAYERS)
    ]
    unit_rows = (
        picked(spread[:, :, narrow:].reshape(owners, LAYERS, 2, unit_half), core, 2)
        .swapaxes(0, 1)
        .reshape(LAYERS, units // 2)
        .astype(F32)
    )

    shards = {}
    for layer in range(LAYERS):
        shards["branch", layer] = jnp.concatenate(
            [
                half_columns(query_weight[layer]),
                half_columns(key_weight[layer]),
                half_columns(value_weight[layer]),
                half_columns(output_weight[layer]),
            ],
            1,
        )
        shards["up", layer] = picked(
            up_weight[layer].reshape(shard, owners, 2, unit_half), core, 2
        ).reshape(shard, units // 2)
        shards["down", layer] = lax.dynamic_slice_in_dim(
            down_weight[layer], core * unit_half, unit_half, 0
        )
    gathered = {}
    if direct:
        earlier = [None] * 3
        for kind, layer in GATHER_ORDER:
            if kind == "branch":
                piece = shards["branch", layer]
            else:
                up_piece = picked(
                    shards["up", layer].reshape(2, shard // 2, units // 2), side, 0
                )
                down_piece = picked(
                    shards["down", layer].reshape(2, 2, shard // 2, features), side, 0
                )
                down_piece = jnp.concatenate([down_piece[0], down_piece[1]], -1)
                piece = jnp.concatenate([up_piece, down_piece], 0)
            near = piece[None]
            for position, step in enumerate(LINE_STEPS):
                if earlier[position] is not None:
                    near = after(near, earlier[position])
                near = doubled(near, step)
                earlier[position] = near
            if earlier[2] is not None:
                near = after(near, earlier[2])
            far = swap_pair(near)
            earlier[2] = far
            if kind == "branch":
                (gathered["in", layer],) = place(
                    fill_in,
                    where,
                    ((near, 3 * half, 0), (far, 3 * half, 0)),
                    ((2, shard, 3 * half),),
                    "place_in",
                )
                gathered["in", layer] = gathered["in", layer].reshape(features, 3 * half)
                swapped = swap_core(
                    jnp.concatenate([near[:, :, 3 * half :], far[:, :, 3 * half :]], 2)
                )
                (gathered["out", layer],) = place(
                    fill_out,
                    where,
                    ((near, half, 3), (far, half, 3), (swapped, half, 0), (swapped, half, 1)),
                    ((2, shard, features),),
                    "place_out",
                )
                gathered["out", layer] = gathered["out", layer].reshape(features, features)
            else:
                width = 2 * features
                gathered["up", layer], gathered["down", layer] = place(
                    fill_wide,
                    where,
                    tuple((v, width, 0) for v in (near, far, swap_row(near), swap_row(far))),
                    ((2, 2, shard // 2, width), (2, 2, 2, shard // 2, features)),
                    "place_wide",
                )
                gathered["up", layer] = gathered["up", layer].reshape(features, units // 2)
                gathered["down", layer] = gathered["down", layer].reshape(units // 2, features)
    else:
        for layer in range(LAYERS):
            for kind in ("up", "down"):
                gathered[kind, layer] = lax.all_gather(
                    shards[kind, layer], "wt", axis=0, tiled=True
                )
            branch = lax.all_gather(shards["branch", layer], "wt", axis=0, tiled=True)
            gathered["in", layer] = branch[:, : 3 * half]
            out_half = branch[:, 3 * half :]
            gathered["out", layer] = by_core(core, out_half, swap_core(out_half), 1)
    weights = [
        tuple(gathered[kind, layer] for kind in ("in", "out", "up", "down"))
        for layer in range(LAYERS)
    ]

    hidden = to_chip(activations).astype(F32)
    kept = []
    for layer in range(LAYERS):
        vec = vectors[layer]
        in_weight, out_weight, up, down = weights[layer]
        flat, _ = norm_parts(hidden)
        normed = (flat * vec["first_scale"] + vec["first_shift"]).astype(BF)
        in_bias = jnp.concatenate(
            [
                lax.dynamic_slice_in_dim(vec["query_bias"], core * half, half, 0),
                jnp.zeros((half,), F32),
                lax.dynamic_slice_in_dim(vec["value_bias"], core * half, half, 0),
            ]
        )
        qkv = (matmul(normed, in_weight) + in_bias).astype(BF)
        mixture_half = attend(qkv)
        mixture = by_core(core, mixture_half, swap_core(mixture_half), 1)
        middle = hidden + matmul(mixture, out_weight) + vec["output_bias"]
        flat, _ = norm_parts(middle)
        second = (flat * vec["second_scale"] + vec["second_shift"]).astype(BF)
        upward = matmul(second, up) + unit_rows[layer]
        activated, slope = gelu_parts(upward)
        activated = activated.astype(BF)
        slope = slope.astype(BF)
        kept.append((hidden, normed, qkv, mixture, middle, second, activated, slope))
        partial = matmul(activated, down)
        if layer + 1 < LAYERS:
            hidden = middle + vec["down_bias"] + (partial + swap_core(partial.astype(BF)))
        else:
            theirs = lax.dynamic_slice_in_dim(
                partial, (1 - core) * 2 * frames_here, 2 * frames_here, 0
            )
            total = own_rows(partial) + swap_core(theirs.astype(BF))
            result_rows = (own_rows(middle) + vec["down_bias"] + total).astype(BF)

    grad_hidden = to_chip(upstream).astype(F32)
    settled = [None] * LAYERS
    vector_grads = [None] * LAYERS
    for layer in reversed(range(LAYERS)):
        vec = vectors[layer]
        in_weight, out_weight, up, down = weights[layer]
        hidden, normed, qkv, mixture, middle, second, activated, slope = kept[layer]
        grads = {}
        down_in = grad_hidden.astype(BF)
        grad_down = left_product(activated, down_in).astype(BF)
        grad_down = grad_down.reshape(owners, 2, 2, unit_half // 4, features)
        down_sent = picked(grad_down, 1 - side, 1)
        down_there = swap_row(jnp.concatenate([down_sent[:, 0], down_sent[:, 1]], -1))
        grads["down_bias"] = column_sums(down_in)
        grad_upward = (slope.astype(F32) * right_product(down_in, down)).astype(BF)
        grad_up = left_product(second, grad_upward).astype(BF)
        grad_up = grad_up.reshape(owners, 2, shard // 2, units // 2)
        up_there = swap_row(picked(grad_up, 1 - side, 1))
        down_kept = picked(grad_down, side, 1)
        down_kept = jnp.concatenate([down_kept[:, 0], down_kept[:, 1]], -1)
        grad_wide = reduce_owners(
            jnp.concatenate(
                [
                    (picked(grad_up, side, 1).astype(F32) + up_there.astype(F32)).astype(BF),
                    (down_kept.astype(F32) + down_there.astype(F32)).astype(BF),
                ],
                1,
            )
        )
        grad_up_bias = column_sums(grad_upward)
        partial = right_product(grad_upward, up)
        grad_second = partial + swap_core(partial.astype(BF))
        before, grads["second_scale"], grads["second_shift"] = norm_back(
            middle, vec["second_scale"], grad_second
        )
        grad_middle = grad_hidden + before
        branch_in = grad_middle.astype(BF)
        grads["output_bias"] = column_sums(branch_in)
        grad_out = left_product(mixture, half_columns(branch_in))
        out_rows = lax.dynamic_slice_in_dim(out_weight, core * half, half, 0)
        grad_mixture = right_product(branch_in, out_rows).astype(BF)
        grad_qkv = jnp.concatenate(attend_back(qkv, grad_mixture), 1)
        grad_in = left_product(normed, grad_qkv)
        grad_branch = jnp.concatenate([grad_in.astype(BF), grad_out.astype(BF)], 1)
        grad_branch = reduce_owners(grad_branch.reshape(owners, shard, 2 * features))
        grad_in_bias = column_sums(grad_qkv)
        partial = right_product(grad_qkv, in_weight)
        if layer == 0:
            result_rows = after(result_rows, grad_qkv)
            result = from_chip(result_rows)
        if layer > 0:
            grad_normed = partial + swap_core(partial.astype(BF))
            before, grads["first_scale"], grads["first_shift"] = norm_back(
                hidden, vec["first_scale"], grad_normed
            )
            grad_hidden = grad_middle + before
        else:
            theirs = lax.dynamic_slice_in_dim(
                partial, (1 - core) * 2 * frames_here, 2 * frames_here, 0
            )
            grad_normed = own_rows(partial) + swap_core(theirs.astype(BF))
            before, grads["first_scale"], grads["first_shift"] = norm_back(
                own_rows(hidden), vec["first_scale"], grad_normed
            )
            input_grad = from_chip(own_rows(grad_middle) + before)

        grads["query_bias"] = grad_in_bias[:half]
        grads["value_bias"] = grad_in_bias[2 * half :]
        blank = jnp.zeros((half,), F32)
        rows = []
        for name in VECTORS:
            values = grads[name]
            if name in ("query_bias", "value_bias"):
                values = jnp.where(
                    core == 0,
                    jnp.concatenate([values, blank]),
                    jnp.concatenate([blank, values]),
                )
            elif layer > 0 or name not in ("first_scale", "first_shift"):
                values = jnp.where(core == 0, values, 0.0)
            rows.append(values)
        vector_grads[layer] = (jnp.stack(rows), grad_up_bias)
        done = {}
        sent = jnp.concatenate([grad_branch, grad_wide], 0).astype(BF)
        other = swap_row(sent)
        grad_branch = (grad_branch + other[:shard].astype(F32)).astype(BF)
        wide, wide_there = sent[shard:], other[shard:]
        wide = jnp.where(
            side == 0, jnp.stack([wide, wide_there]), jnp.stack([wide_there, wide])
        ).reshape(2 * shard, 2 * features)
        mine = jnp.concatenate([grad_branch, wide], 0)
        other = swap_core(mine)
        low = jnp.where(core == 0, mine, other).astype(F32)
        high = jnp.where(core == 0, other, mine).astype(F32)
        for position, name in enumerate(
            ("query_weight", "key_weight", "value_weight", "output_weight")
        ):
            part = slice(position * half, (position + 1) * half)
            done[name] = jnp.concatenate([low[:shard, part], high[:shard, part]], 1)

        def up_part(values):
            values = values[shard:].reshape(2, 2, shard // 2, units // 2)[:, 0]
            return values.reshape(shard, owners, unit_half)

        def down_part(values):
            values = values[shard:].reshape(2, 2, unit_half // 4, units // 2)[:, 1]
            values = values.reshape(2, unit_half // 4, 2, features)
            return jnp.swapaxes(values, 1, 2).reshape(unit_half, features)

        done["up_weight"] = jnp.stack([up_part(low), up_part(high)], 2).reshape(shard, units)
        done["down_weight"] = jnp.concatenate([down_part(low), down_part(high)], 0)
        settled[layer] = done

    packed = jnp.stack([rows for rows, _ in vector_grads])
    packed = packed.reshape(LAYERS * len(VECTORS), owners, shard).swapaxes(0, 1)
    packed = packed.reshape(owners, LAYERS * narrow)
    from_units = jnp.stack([values for _, values in vector_grads])
    from_units = from_units.reshape(LAYERS, owners, unit_half).swapaxes(0, 1)
    from_units = from_units.reshape(owners, LAYERS * unit_half)
    packed = reduce_owners(jnp.concatenate([packed, from_units], 1), F32)
    packed = packed + swap_row(packed)
    other = swap_core(packed)
    narrow_sum = (packed + other)[: LAYERS * narrow].reshape(LAYERS, len(VECTORS), shard)
    unit_mine = packed[LAYERS * narrow :].reshape(LAYERS, unit_half)
    unit_other = other[LAYERS * narrow :].reshape(LAYERS, unit_half)
    summed = {name: narrow_sum[:, position] for position, name in enumerate(VECTORS)}
    summed["up_bias"] = by_core(core, unit_mine, unit_other, 1)

    names = (
        "first_scale",
        "first_shift",
        "query_weight",
        "query_bias",
        "key_weight",
        "value_weight",
        "value_bias",
        "output_weight",
        "output_bias",
        "second_scale",
        "second_shift",
        "up_weight",
        "up_bias",
        "down_weight",
        "down_bias",
    )
    final = tuple(
        summed[name]
        if name in summed
        else jnp.stack([settled[layer][name] for layer in range(LAYERS)])
        for name in names
    )
    return (result, input_grad) + final


def solution(mesh):
    rows, vector, matrix = P("wt", "seq", None), P(None, "wt"), P(None, "wt", None)
    parameters = (
        vector,
        vector,
        matrix,
        vector,
        matrix,
        matrix,
        vector,
        matrix,
        vector,
        vector,
        vector,
        matrix,
        vector,
        matrix,
        vector,
    )
    specs = (rows, rows) + parameters
    return jax.shard_map(
        per_device, mesh=mesh, in_specs=specs, out_specs=specs, check_vma=False
    )
```

```python
import math

import jax
import jax.numpy as jnp
from jax import lax
from jax.experimental import pallas as pl
from jax.experimental.pallas import tpu as pltpu
from jax.sharding import PartitionSpec as P

HEAD_DIM = 64
LAYERS = 2
epsilon = 1e-05
BF = jnp.bfloat16
F32 = jnp.float32
VMEM_BYTES = 48 * 1024 * 1024

VECTORS = (
    "first_scale",
    "first_shift",
    "query_bias",
    "value_bias",
    "output_bias",
    "second_scale",
    "second_shift",
    "down_bias",
)
LINE_STEPS = (1, 2)


def lasting(microseconds):
    return pl.CostEstimate(
        flops=int(microseconds * 1.15e9),
        bytes_accessed=int(microseconds * 3.69e6),
        transcendentals=0,
    )


def matmul(left, right):
    return jnp.dot(left, right, preferred_element_type=F32)


def left_product(left, right):
    return lax.dot_general(left, right, (((0,), (0,)), ((), ())), preferred_element_type=F32)


def right_product(left, right):
    return lax.dot_general(left, right, (((1,), (1,)), ((), ())), preferred_element_type=F32)


def column_sums(values):
    return jnp.sum(values, axis=0, dtype=F32)


def swap_core(values):
    pairs = [(i, i ^ 1) for i in range(lax.axis_size("seq"))]
    return lax.ppermute(values, "seq", pairs)


def swap_row(values):
    pairs = [(i, i ^ 2) for i in range(lax.axis_size("seq"))]
    return lax.ppermute(values, "seq", pairs)


def by_core(core, mine, theirs, axis):
    return jnp.where(
        core == 0,
        jnp.concatenate([mine, theirs], axis),
        jnp.concatenate([theirs, mine], axis),
    )


def swap_pair(values):
    pairs = [(i, i ^ 1) for i in range(lax.axis_size("wt"))]
    return lax.ppermute(values, "wt", pairs)


def picked(values, index, axis):
    return lax.dynamic_index_in_dim(values, index, axis, keepdims=False)


def after(values, earlier):
    return lax.optimization_barrier((values, earlier))[0]


def swap_line(values, step):
    pairs = [(i, i ^ (2 * step)) for i in range(lax.axis_size("wt"))]
    return lax.ppermute(values, "wt", pairs)


def doubled(values, step):
    return jnp.concatenate([values, swap_line(values, step)], 0)


def place_kernel(fill, where_ref, *refs):
    fill(where_ref, *refs)


def place(fill, where, sources, spots, name):
    depth = sources[0][0].shape[0]
    rows = sources[0][0].shape[1]
    size = sum(math.prod(spot) for spot in spots) * depth

    def spot_index(spot):
        blank = (0,) * len(spot)
        return lambda k, w: (jnp.bitwise_xor(w[0], k),) + blank

    return pl.pallas_call(
        lambda *refs: place_kernel(fill, *refs),
        grid_spec=pltpu.PrefetchScalarGridSpec(
            num_scalar_prefetch=1,
            grid=(depth,),
            in_specs=[
                pl.BlockSpec((1, rows, width), lambda k, w, block=block: (k, 0, block))
                for _, width, block in sources
            ],
            out_specs=[pl.BlockSpec((1,) + spot, spot_index(spot)) for spot in spots],
        ),
        out_shape=[jax.ShapeDtypeStruct((depth,) + spot, BF) for spot in spots],
        compiler_params=pltpu.CompilerParams(vmem_limit_bytes=VMEM_BYTES),
        cost_estimate=lasting(3.0),
        name=name,
    )(where, *(array for array, _, _ in sources))


def piece_spots(where_ref, count):
    spots = [(0, where_ref[1]), (0, 1 - where_ref[1])]
    if count == 2:
        return spots
    return [spot + (where_ref[2],) for spot in spots] + [
        spot + (1 - where_ref[2],) for spot in spots
    ]


def fill_in(where_ref, *refs):
    sources, target = refs[:-1], refs[-1]
    for spot, source in zip(piece_spots(where_ref, len(sources)), sources):
        target[spot] = source[0]


def fill_out(where_ref, *refs):
    sources, target = refs[:-1], refs[-1]
    count = len(sources) // 2
    width = sources[0].shape[-1]
    here = pl.ds(pl.multiple_of(where_ref[3] * width, 128), width)
    there = pl.ds(pl.multiple_of((1 - where_ref[3]) * width, 128), width)
    for columns, group in ((here, sources[:count]), (there, sources[count:])):
        for spot, source in zip(piece_spots(where_ref, count), group):
            target[spot + (slice(None), columns)] = source[0]


def fill_wide(where_ref, near_ref, far_ref, near_there_ref, far_there_ref, up, down):
    rows = near_ref.shape[1] // 2
    features = down.shape[-1]
    for source, across, over in (
        (near_ref, where_ref[1], where_ref[2]),
        (far_ref, 1 - where_ref[1], where_ref[2]),
        (near_there_ref, where_ref[1], 1 - where_ref[2]),
        (far_there_ref, 1 - where_ref[1], 1 - where_ref[2]),
    ):
        up[0, across, over] = source[0, :rows]
        down[0, across, over, 0] = source[0, rows:, :features]
        down[0, across, over, 1] = source[0, rows:, features:]


class Reducer:
    def __init__(self):
        self.arrived = None
        self.stages = [None, None, None]
        self.totals = []

    def tick(self, values=None, gate=None, beside=None):
        owners = lax.axis_size("wt")
        if owners != 8:
            if values is not None:
                self.totals.append(
                    [
                        lax.psum_scatter(v, "wt", scatter_dimension=0, tiled=False).astype(F32)
                        for v in values
                    ]
                )
            return None if beside is None else swap_row(beside)
        own = lax.axis_index("wt")
        bits = (own % 2, own // 4, own // 2 % 2)
        moves = (swap_pair, lambda v: swap_line(v, 2), lambda v: swap_line(v, 1))
        axes = (1, 0, 0)
        if values is not None:
            self.stages[0] = [v.reshape((owners // 2, 2) + v.shape[1:]) for v in values]
        active = [i for i in range(3) if self.stages[i] is not None]
        sends = [[picked(v, 1 - bits[i], axes[i]) for v in self.stages[i]] for i in active]
        earlier = [v for v in (self.arrived, gate) if v is not None]
        if earlier:
            sends, beside = after((sends, beside), earlier)
        theirs = [[moves[i](v) for v in send] for i, send in zip(active, sends)]
        swapped = None if beside is None else swap_row(beside)
        self.arrived = (theirs, swapped)
        following = [None, None, None]
        for i, there in zip(active, theirs):
            kept = [picked(v, bits[i], axes[i]) for v in self.stages[i]]
            total = [k.astype(F32) + t.astype(F32) for k, t in zip(kept, there)]
            if i == 2:
                self.totals.append(total)
                continue
            total = [v.astype(k.dtype) for v, k in zip(total, kept)]
            if i == 0:
                total = [v.reshape((2, 2) + v.shape[1:]) for v in total]
            following[i + 1] = total
        self.stages = following
        return swapped

    def finish(self):
        while any(stage is not None for stage in self.stages):
            self.tick()


def attend_kernel(q_ref, k_ref, v_ref, o_ref):
    factor = 1.0 / math.sqrt(HEAD_DIM)
    for head in range(q_ref.shape[1] // HEAD_DIM):
        part = slice(head * HEAD_DIM, (head + 1) * HEAD_DIM)
        scores = right_product(q_ref[:, part], k_ref[:, part]) * factor
        raised = jnp.exp(scores - jnp.max(scores, axis=1, keepdims=True))
        chances = raised * (1.0 / jnp.sum(raised, axis=1, keepdims=True))
        o_ref[:, part] = matmul(chances.astype(BF), v_ref[:, part]).astype(BF)


def attend(qkv):
    rows, width = qkv.shape
    width //= 3
    block = 2 * HEAD_DIM
    steps = width // block
    return pl.pallas_call(
        attend_kernel,
        grid=(steps,),
        in_specs=[
            pl.BlockSpec((rows, block), lambda i: (0, i)),
            pl.BlockSpec((rows, block), lambda i: (0, steps + i)),
            pl.BlockSpec((rows, block), lambda i: (0, 2 * steps + i)),
        ],
        out_specs=pl.BlockSpec((rows, block), lambda i: (0, i)),
        out_shape=jax.ShapeDtypeStruct((rows, width), BF),
        compiler_params=pltpu.CompilerParams(vmem_limit_bytes=VMEM_BYTES),
        cost_estimate=lasting(6.0),
        name="attend",
    )(qkv, qkv, qkv)


def attend_back_kernel(q_ref, k_ref, v_ref, eo_ref, eq_ref, ek_ref, ev_ref):
    factor = 1.0 / math.sqrt(HEAD_DIM)
    for head in range(q_ref.shape[1] // HEAD_DIM):
        part = slice(head * HEAD_DIM, (head + 1) * HEAD_DIM)
        queries, keys, eo = q_ref[:, part], k_ref[:, part], eo_ref[:, part]
        scores = right_product(keys, queries) * factor
        raised = jnp.exp(scores - jnp.max(scores, axis=0, keepdims=True))
        chances = raised * (1.0 / jnp.sum(raised, axis=0, keepdims=True))
        ep = right_product(v_ref[:, part], eo)
        ev_ref[:, part] = matmul(chances.astype(BF), eo).astype(BF)
        inner = jnp.sum(ep * chances, axis=0, keepdims=True)
        es = (chances * (ep - inner)).astype(BF)
        ek_ref[:, part] = (matmul(es, queries) * factor).astype(BF)
        eq_ref[:, part] = (left_product(keys, es) * factor).T.astype(BF)


def attend_back(qkv, eo):
    rows, width = eo.shape
    block = 2 * HEAD_DIM
    steps = width // block
    return pl.pallas_call(
        attend_back_kernel,
        grid=(steps,),
        in_specs=[
            pl.BlockSpec((rows, block), lambda i: (0, i)),
            pl.BlockSpec((rows, block), lambda i: (0, steps + i)),
            pl.BlockSpec((rows, block), lambda i: (0, 2 * steps + i)),
            pl.BlockSpec((rows, block), lambda i: (0, i)),
        ],
        out_specs=[pl.BlockSpec((rows, block), lambda i: (0, i))] * 3,
        out_shape=[jax.ShapeDtypeStruct((rows, width), BF)] * 3,
        compiler_params=pltpu.CompilerParams(vmem_limit_bytes=VMEM_BYTES),
        cost_estimate=lasting(8.2),
        name="attend_back",
    )(qkv, qkv, qkv, eo)


def norm_parts(values):
    centred = values - jnp.mean(values, axis=-1, keepdims=True)
    spread = jnp.mean(centred * centred, axis=-1, keepdims=True)
    rate = lax.rsqrt(spread + epsilon)
    return centred * rate, rate


def pack_kernel(where_ref, *refs):
    *squares, up_ref, down_ref, branch_ref, wide_ref = refs
    side, core = where_ref[2], where_ref[3]
    shard, features = squares[0].shape[1:]
    half, part = features // 2, shard // 2
    unit_half = down_ref.shape[1] // 2
    columns = pl.ds(pl.multiple_of(core * half, 128), half)
    for position, square in enumerate(squares):
        branch_ref[:, position * half : (position + 1) * half] = square[0, :, columns]
    rows = up_ref[0, pl.ds(pl.multiple_of(side * part, 16), part), :]
    chosen = []
    for owner in range(up_ref.shape[2] // (2 * unit_half)):
        first = 2 * owner * unit_half
        low = rows[:, first : first + unit_half]
        high = rows[:, first + unit_half : first + 2 * unit_half]
        chosen.append(jnp.where(core == 0, low, high))
    wide_ref[:part, :] = jnp.concatenate(chosen, 1)
    for pair in range(2):
        first = pl.multiple_of(core * unit_half + side * shard, 16) + pair * part
        wide_ref[part:, pair * features : (pair + 1) * features] = down_ref[
            0, pl.ds(first, part), :
        ]


def pack(where, squares, up, down, layer):
    members = (*squares, up, down)
    shard, features = squares[0].shape[1:]
    shape = (shard, 2 * features)
    return pl.pallas_call(
        pack_kernel,
        grid=(1,),
        in_specs=[pl.BlockSpec(memory_space=pltpu.SMEM)]
        + [pl.BlockSpec((1,) + v.shape[1:], lambda i: (layer, 0, 0)) for v in members],
        out_specs=[pl.BlockSpec(shape, lambda i: (0, 0))] * 2,
        out_shape=[jax.ShapeDtypeStruct(shape, BF)] * 2,
        compiler_params=pltpu.CompilerParams(vmem_limit_bytes=VMEM_BYTES),
        cost_estimate=lasting(3.0),
        name="pack",
    )(where, *members)


def norm_next_kernel(base_ref, partial_ref, *refs):
    *theirs, bias_ref, scale_ref, shift_ref, value_ref, normed_ref = refs
    value = base_ref[...] + partial_ref[...] + bias_ref[...]
    for there in theirs:
        value = value + there[...].astype(F32)
    value_ref[...] = value
    flat, _ = norm_parts(value)
    normed_ref[...] = (flat * scale_ref[...] + shift_ref[...]).astype(BF)


def norm_next(base, parts, bias, scale, shift):
    rows, features = base.shape
    block = pl.BlockSpec((rows // 4, features), lambda i: (i, 0))
    line = pl.BlockSpec((1, features), lambda i: (0, 0))
    return pl.pallas_call(
        norm_next_kernel,
        grid=(4,),
        in_specs=[block] * (1 + len(parts)) + [line] * 3,
        out_specs=[block] * 2,
        out_shape=[
            jax.ShapeDtypeStruct((rows, features), F32),
            jax.ShapeDtypeStruct((rows, features), BF),
        ],
        compiler_params=pltpu.CompilerParams(vmem_limit_bytes=VMEM_BYTES),
        cost_estimate=lasting(2.9),
        name="norm_next",
    )(base, *parts, *(v.reshape(1, features) for v in (bias, scale, shift)))


def norm_back_kernel(offset_ref, partial_ref, there_ref, value_ref, scale_ref, base_ref, *outs):
    out_ref, low_ref, sums_ref = outs

    @pl.when(pl.program_id(0) == 0)
    def _():
        sums_ref[...] = jnp.zeros_like(sums_ref)

    grad = partial_ref[...] + there_ref[...].astype(F32)
    flat, rate = norm_parts(value_ref[...])
    inner = grad * scale_ref[...]
    mean_inner = jnp.mean(inner, axis=-1, keepdims=True)
    mean_cross = jnp.mean(inner * flat, axis=-1, keepdims=True)
    total = base_ref[...] + rate * (inner - mean_inner - flat * mean_cross)
    out_ref[...] = total
    low = total.astype(BF)
    low_ref[...] = low
    sums_ref[0:1] += jnp.sum(grad * flat, axis=0, keepdims=True)
    sums_ref[1:2] += jnp.sum(grad, axis=0, keepdims=True)
    sums_ref[2:3] += jnp.sum(low.astype(F32), axis=0, keepdims=True)


def norm_back(partial, there, value, scale, base, offset):
    rows, features = there.shape
    block = rows // 4
    steps = rows // block
    moved = pl.BlockSpec((block, features), lambda i, w: (w[0] * steps + i, 0))
    plain = pl.BlockSpec((block, features), lambda i, w: (i, 0))
    return pl.pallas_call(
        norm_back_kernel,
        grid_spec=pltpu.PrefetchScalarGridSpec(
            num_scalar_prefetch=1,
            grid=(steps,),
            in_specs=[
                moved,
                plain,
                moved,
                pl.BlockSpec((1, features), lambda i, w: (0, 0)),
                moved,
            ],
            out_specs=[plain, plain, pl.BlockSpec((8, features), lambda i, w: (0, 0))],
        ),
        out_shape=[
            jax.ShapeDtypeStruct((rows, features), F32),
            jax.ShapeDtypeStruct((rows, features), BF),
            jax.ShapeDtypeStruct((8, features), F32),
        ],
        compiler_params=pltpu.CompilerParams(vmem_limit_bytes=VMEM_BYTES),
        cost_estimate=lasting(3.8),
        name="norm_back",
    )(offset, partial, there, value, scale.reshape(1, features), base)


def gelu_parts(values):
    below = 0.5 * (1.0 + lax.erf(values * math.sqrt(0.5)))
    density = jnp.exp(-0.5 * values * values) * (1.0 / math.sqrt(2.0 * math.pi))
    return values * below, below + values * density


def settle_kernel(core_ref, mine_ref, mine_wide_ref, other_ref, other_wide_ref, *refs):
    *squares, up, down = refs[-6:]
    core = core_ref[0]
    shard, features = squares[0].shape[1:]
    half = features // 2
    unit_half = down.shape[1] // 2
    owners = up.shape[2] // (2 * unit_half)
    here = pl.ds(pl.multiple_of(core * half, 128), half)
    there = pl.ds(pl.multiple_of((1 - core) * half, 128), half)
    for position, target in enumerate(squares):
        columns = slice(position * half, (position + 1) * half)
        target[0, :, here] = mine_ref[:, columns].astype(F32)
        target[0, :, there] = other_ref[:, columns].astype(F32)
    mine, other = mine_wide_ref[:shard].astype(F32), other_wide_ref[:shard].astype(F32)
    low = jnp.where(core == 0, mine, other)
    high = jnp.where(core == 0, other, mine)
    for owner in range(owners):
        columns = slice(owner * unit_half, (owner + 1) * unit_half)
        up[0, :, 2 * owner * unit_half : 2 * (owner + 1) * unit_half] = jnp.concatenate(
            [low[:, columns], high[:, columns]], 1
        )
    for pair in range(2):
        columns = slice(pair * features, (pair + 1) * features)
        for source, where in ((mine_wide_ref, core), (other_wide_ref, 1 - core)):
            rows = pl.ds(pl.multiple_of(where * unit_half, 8) + pair * shard, shard)
            down[0, rows] = source[shard:, columns].astype(F32)


def settle(core, pieces, earlier, layer, shapes):
    size = sum(math.prod(shape[1:]) for shape in shapes)
    return pl.pallas_call(
        settle_kernel,
        grid=(1,),
        in_specs=[pl.BlockSpec(memory_space=pltpu.SMEM)]
        + [pl.BlockSpec(piece.shape, lambda i: (0, 0)) for piece in pieces]
        + [pl.BlockSpec(memory_space=pl.ANY)] * len(earlier),
        out_specs=[
            pl.BlockSpec((1,) + shape[1:], lambda i: (layer, 0, 0)) for shape in shapes
        ],
        out_shape=[jax.ShapeDtypeStruct(shape, F32) for shape in shapes],
        input_output_aliases={1 + len(pieces) + i: i for i in range(len(earlier))},
        compiler_params=pltpu.CompilerParams(vmem_limit_bytes=VMEM_BYTES),
        cost_estimate=lasting(2.0),
        name="settle",
    )(core, *pieces, *earlier)


def per_device(
    activations,
    upstream,
    first_scale,
    first_shift,
    query_weight,
    query_bias,
    key_weight,
    value_weight,
    value_bias,
    output_weight,
    output_bias,
    second_scale,
    second_shift,
    up_weight,
    up_bias,
    down_weight,
    down_bias,
):
    owners = lax.axis_size("wt")
    seat = lax.axis_index("seq")
    core, side = seat % 2, seat // 2
    frames_here, features = activations.shape[1:]
    half = features // 2
    shard = features // owners
    units = up_weight.shape[2]
    unit_shard = units // owners
    unit_half = unit_shard // 2

    def to_chip(values):
        kept = lax.dynamic_index_in_dim(values, side, 0, keepdims=False)
        sent = lax.dynamic_index_in_dim(values, 1 - side, 0, keepdims=False)
        mine = jnp.concatenate([kept, swap_row(sent)], 0)
        return by_core(core, mine, swap_core(mine), 0)

    def from_chip(mine):
        kept, sent = mine[:frames_here], mine[frames_here:]
        other = swap_row(sent)
        return jnp.where(side == 0, jnp.stack([kept, other]), jnp.stack([other, kept]))

    def own_rows(values):
        return lax.dynamic_slice_in_dim(values, core * 2 * frames_here, 2 * frames_here, 0)

    def half_columns(values):
        return lax.dynamic_slice_in_dim(values, core * half, half, 1)

    direct = owners == 8
    own = lax.axis_index("wt")
    line, across = own // 2, own % 2
    where = jnp.stack([line, across, side, core]).astype(jnp.int32)

    down_in = to_chip(upstream)
    shards = {}
    for layer in range(LAYERS):
        shards["branch", layer] = jnp.concatenate(
            [
                half_columns(query_weight[layer]),
                half_columns(key_weight[layer]),
                half_columns(value_weight[layer]),
                half_columns(output_weight[layer]),
            ],
            1,
        )
    for layer in range(LAYERS):
        shards["up", layer] = picked(
            up_weight[layer].reshape(shard, owners, 2, unit_half), core, 2
        ).reshape(shard, units // 2)
        shards["down", layer] = lax.dynamic_slice_in_dim(
            down_weight[layer], core * unit_half, unit_half, 0
        )
    members = dict(
        first_scale=first_scale,
        first_shift=first_shift,
        query_bias=query_bias,
        value_bias=value_bias,
        output_bias=output_bias,
        second_scale=second_scale,
        second_shift=second_shift,
        down_bias=down_bias,
    )
    narrow = len(VECTORS) * shard
    packed = jnp.concatenate([members[name] for name in VECTORS] + [up_bias], 1)
    gathered = {}
    if direct:

        squares = (query_weight, key_weight, value_weight, output_weight)
        branch_piece, wide_piece = zip(
            *(pack(where, squares, up_weight, down_weight, layer) for layer in range(LAYERS))
        )

        wide_hop = doubled(wide_piece[0][None], 1)
        hop = doubled(after(branch_piece[0], wide_hop)[None], 1)
        wide = [doubled(wide_hop, 2), None]
        packed = after(packed, wide[0])
        wide_near, hop, piece = after(
            (wide[0], hop, wide_piece[1][None]), (wide[0], down_in)
        )
        wide_far = [swap_pair(wide_near), None]
        wide_there = [swap_row(wide_near), None]
        branch = [doubled(hop, 2), None]
        wide_hop = doubled(piece, 1)
        near, far, hop, piece = after(
            (branch[0], wide_far[0], wide_hop, branch_piece[1]),
            (wide_far[0], wide_there[0], branch[0]),
        )
        branch_far = [swap_pair(near), None]
        wide_far_there = [swap_row(far), None]
        wide[1] = doubled(hop, 2)
        hop = doubled(piece[None], 1)
        near, hop = after((wide[1], hop), (branch_far[0], wide_far_there[0], wide[1]))
        wide_far[1] = swap_pair(near)
        wide_there[1] = swap_row(near)
        branch[1] = doubled(hop, 2)
        third = (wide_far[1], wide_there[1], branch[1])
        near, far = after((branch[1], wide_far[1]), third)
        branch_far[1], wide_far_there[1] = lax.optimization_barrier(
            (swap_pair(near), swap_row(far))
        )

        for layer in range(LAYERS):
            pieces = (branch[layer], branch_far[layer])
            (gathered["in", layer],) = place(
                fill_in,
                where,
                tuple((v, 3 * half, 0) for v in pieces),
                ((2, shard, 3 * half),),
                "place_in",
            )
            gathered["in", layer] = gathered["in", layer].reshape(features, 3 * half)
            swapped = swap_core(jnp.concatenate([v[:, :, 3 * half :] for v in pieces], 2))
            (gathered["out", layer],) = place(
                fill_out,
                where,
                tuple((v, half, 3) for v in pieces) + ((swapped, half, 0), (swapped, half, 1)),
                ((2, shard, features),),
                "place_out",
            )
            gathered["out", layer] = gathered["out", layer].reshape(features, features)
            width = 2 * features
            pieces = (wide[layer], wide_far[layer], wide_there[layer], wide_far_there[layer])
            gathered["up", layer], gathered["down", layer] = place(
                fill_wide,
                where,
                tuple((v, width, 0) for v in pieces),
                ((2, 2, shard // 2, width), (2, 2, 2, shard // 2, features)),
                "place_wide",
            )
            gathered["up", layer] = gathered["up", layer].reshape(features, units // 2)
            gathered["down", layer] = gathered["down", layer].reshape(units // 2, features)
    else:
        for layer in range(LAYERS):
            for kind in ("up", "down"):
                gathered[kind, layer] = lax.all_gather(
                    shards[kind, layer], "wt", axis=0, tiled=True
                )
            branch = lax.all_gather(shards["branch", layer], "wt", axis=0, tiled=True)
            gathered["in", layer] = branch[:, : 3 * half]
            out_half = branch[:, 3 * half :]
            gathered["out", layer] = by_core(core, out_half, swap_core(out_half), 1)
    if direct:
        reached = packed[None]
        for step in LINE_STEPS:
            reached = doubled(reached, step)
        other = swap_pair(reached)
        spread = jnp.stack([reached, other], 1)
        for bit in LINE_STEPS:
            turned = spread.reshape((owners // (4 * bit), 2, bit, 2) + packed.shape)
            spread = jnp.where((line & bit) == 0, turned, turned[:, ::-1]).reshape(spread.shape)
        spread = jnp.where(across == 0, spread, spread[:, ::-1]).reshape(
            (owners,) + packed.shape
        )
    else:
        spread = lax.all_gather(packed, "wt", axis=0, tiled=False)
    vector_rows = (
        spread[:, :, :narrow]
        .reshape(owners, LAYERS * len(VECTORS), shard)
        .swapaxes(0, 1)
        .reshape(LAYERS * len(VECTORS), features)
        .astype(F32)
    )
    vectors = [
        {
            name: vector_rows[layer * len(VECTORS) + position]
            for position, name in enumerate(VECTORS)
        }
        for layer in range(LAYERS)
    ]
    unit_rows = (
        picked(spread[:, :, narrow:].reshape(owners, LAYERS, 2, unit_half), core, 2)
        .swapaxes(0, 1)
        .reshape(LAYERS, units // 2)
        .astype(F32)
    )

    weights = [
        tuple(gathered[kind, layer] for kind in ("in", "out", "up", "down"))
        for layer in range(LAYERS)
    ]

    hidden = to_chip(activations).astype(F32)
    kept = []
    for layer in range(LAYERS):
        vec = vectors[layer]
        in_weight, out_weight, up, down = weights[layer]
        if layer == 0:
            flat, _ = norm_parts(hidden)
            normed = (flat * vec["first_scale"] + vec["first_shift"]).astype(BF)
        in_bias = jnp.concatenate(
            [
                lax.dynamic_slice_in_dim(vec["query_bias"], core * half, half, 0),
                jnp.zeros((half,), F32),
                lax.dynamic_slice_in_dim(vec["value_bias"], core * half, half, 0),
            ]
        )
        qkv = (matmul(normed, in_weight) + in_bias).astype(BF)
        mixture_half = attend(qkv)
        mixture = by_core(core, mixture_half, swap_core(mixture_half), 1)
        middle, second = norm_next(
            hidden,
            (matmul(mixture, out_weight),),
            vec["output_bias"],
            vec["second_scale"],
            vec["second_shift"],
        )
        upward = matmul(second, up) + unit_rows[layer]
        activated, slope = gelu_parts(upward)
        activated = activated.astype(BF)
        if direct and layer == 0:
            activated = after(activated, third)
        slope = slope.astype(BF)
        kept.append((hidden, normed, qkv, mixture, middle, second, activated, slope))
        partial = matmul(activated, down)
        if layer + 1 < LAYERS:
            hidden, normed = norm_next(
                middle,
                (partial, swap_core(partial.astype(BF))),
                vec["down_bias"],
                vectors[layer + 1]["first_scale"],
                vectors[layer + 1]["first_shift"],
            )
        else:
            theirs = lax.dynamic_slice_in_dim(
                partial, (1 - core) * 2 * frames_here, 2 * frames_here, 0
            )
            total = own_rows(partial) + swap_core(theirs.astype(BF))
            result_rows = (own_rows(middle) + vec["down_bias"] + total).astype(BF)

    grad_hidden = down_in.astype(F32)
    grad_down_bias = column_sums(down_in)[None]
    vector_grads = [None] * LAYERS
    settled = ()
    reducer = Reducer()
    row_core = core.reshape(1).astype(jnp.int32)
    no_offset = jnp.zeros((1,), jnp.int32)
    matrix_shapes = tuple(
        (LAYERS,) + shape
        for shape in ((shard, features),) * 4 + ((shard, units), (unit_shard, features))
    )
    for layer in reversed(range(LAYERS)):
        vec = vectors[layer]
        in_weight, out_weight, up, down = weights[layer]
        hidden, normed, qkv, mixture, middle, second, activated, slope = kept[layer]
        grad_down = left_product(activated, down_in).astype(BF)
        grad_upward = (slope.astype(F32) * right_product(down_in, down)).astype(BF)
        grad_up = left_product(second, grad_upward).astype(BF)
        if layer > 0:
            grad_up = grad_up.reshape(owners, shard, units // 2)
            reducer.tick([grad_down.reshape(owners, unit_half, features)])
        else:
            grad_up = grad_up.reshape(owners, 2, shard // 2, units // 2)
            grad_down = grad_down.reshape(owners, 2, 2, shard // 2, features)
            grad_down = jnp.concatenate([grad_down[:, :, 0], grad_down[:, :, 1]], -1)
            down_there = reducer.tick([grad_branch], beside=picked(grad_down, 1 - side, 1))
        grad_up_bias = column_sums(grad_upward)
        partial = right_product(grad_upward, up)
        there = swap_core(partial.astype(BF))
        grad_middle, branch_in, second_sums = norm_back(
            partial, there, middle, vec["second_scale"], grad_hidden, no_offset
        )
        grad_out = left_product(mixture, half_columns(branch_in))
        out_rows = lax.dynamic_slice_in_dim(out_weight, core * half, half, 0)
        grad_mixture = right_product(branch_in, out_rows).astype(BF)
        grad_qkv = jnp.concatenate(attend_back(qkv, grad_mixture), 1)
        grad_in = left_product(normed, grad_qkv).astype(BF)
        grad_branch = jnp.concatenate([grad_in, grad_out.astype(BF)], 1)
        grad_branch = grad_branch.reshape(owners, shard, 2 * features)
        if layer > 0:
            reducer.tick([grad_up], grad_branch)
        else:
            up_there = reducer.tick([grad_branch], beside=picked(grad_up, 1 - side, 1))
            grad_wide = jnp.concatenate(
                [
                    (picked(grad_up, side, 1).astype(F32) + up_there.astype(F32)).astype(BF),
                    (picked(grad_down, side, 1).astype(F32) + down_there.astype(F32)).astype(BF),
                ],
                1,
            )
        grad_in_bias = column_sums(grad_qkv)
        partial = right_product(grad_qkv, in_weight)
        below = grad_down_bias
        if layer > 0:
            there = swap_core(partial.astype(BF))
            grad_hidden, down_in, first_sums = norm_back(
                partial, there, hidden, vec["first_scale"], grad_middle, no_offset
            )
            grad_down_bias = first_sums[2:3]
        else:
            result_rows = after(result_rows, grad_qkv)
            result = from_chip(result_rows)
            theirs = lax.dynamic_slice_in_dim(
                partial, (1 - core) * 2 * frames_here, 2 * frames_here, 0
            )
            there = swap_core(theirs.astype(BF))
            before, _, first_sums = norm_back(
                partial, there, hidden, vec["first_scale"], grad_middle, row_core
            )
            input_grad = from_chip(before)

        twice = jnp.stack([grad_in_bias[:half], grad_in_bias[2 * half :]])
        rows = jnp.concatenate(
            [
                first_sums[:2],
                jnp.concatenate([twice, twice], 1),
                second_sums[2:3],
                second_sums[:2],
                below,
            ],
            0,
        )
        place_row = lax.broadcasted_iota(jnp.int32, rows.shape, 0)
        on_right = lax.broadcasted_iota(jnp.int32, rows.shape, 1) >= half
        counted = jnp.where((place_row == 2) | (place_row == 3), on_right == (core == 1), core == 0)
        if layer == 0:
            counted = counted | (place_row < 2)
        vector_grads[layer] = (jnp.where(counted, rows, 0.0), grad_up_bias)

    packed = jnp.stack([rows for rows, _ in vector_grads])
    packed = packed.reshape(LAYERS * len(VECTORS), owners, shard).swapaxes(0, 1)
    packed = packed.reshape(owners, LAYERS * narrow)
    from_units = jnp.stack([values for _, values in vector_grads])
    from_units = from_units.reshape(LAYERS, owners, unit_half).swapaxes(0, 1)
    from_units = from_units.reshape(owners, LAYERS * unit_half)
    packed = jnp.concatenate([packed, from_units], 1)
    reducer.tick([grad_wide, packed])
    reducer.finish()
    for layer in reversed(range(LAYERS)):
        if layer > 0:
            (grad_down,), (grad_up,), (grad_branch,) = reducer.totals[:3]
            grad_wide = jnp.concatenate(
                [grad_up, jnp.concatenate([grad_down[:shard], grad_down[shard:]], 1)], 0
            )
        else:
            (grad_branch,), (grad_wide, packed) = reducer.totals[3:]

        def over_sides(values):
            values = values.astype(BF)
            values = (values.astype(F32) + swap_row(values).astype(F32)).astype(BF)
            return values, swap_core(values)

        if layer > 0:
            mine, other = over_sides(jnp.concatenate([grad_branch, grad_wide], 0))
            mine, other = (mine[:shard], mine[shard:]), (other[:shard], other[shard:])
        else:
            grad_wide = grad_wide.astype(BF)
            there = swap_row(grad_wide)
            low = jnp.where(side == 0, grad_wide, there)
            high = jnp.where(side == 0, there, grad_wide)
            part = shard // 2
            low_down, high_down = low[part:], high[part:]
            grad_wide = jnp.concatenate(
                [
                    low[:part],
                    high[:part],
                    jnp.concatenate([low_down[:, :features], high_down[:, :features]], 1),
                    jnp.concatenate([low_down[:, features:], high_down[:, features:]], 1),
                ],
                0,
            )
            mine, other = zip(over_sides(grad_branch), (grad_wide, swap_core(grad_wide)))
        if direct:
            settled = settle(row_core, mine + other, settled, layer, matrix_shapes)
            continue
        low = [jnp.where(core == 0, m, o).astype(F32) for m, o in zip(mine, other)]
        high = [jnp.where(core == 0, o, m).astype(F32) for m, o in zip(mine, other)]
        done = []
        for position in range(4):
            part = slice(position * half, (position + 1) * half)
            done.append(jnp.concatenate([low[0][:, part], high[0][:, part]], 1))

        def up_part(values):
            return values[:shard].reshape(shard, owners, unit_half)

        def down_part(values):
            return jnp.concatenate([values[shard:, :features], values[shard:, features:]], 0)

        done.append(jnp.stack([up_part(low[1]), up_part(high[1])], 2).reshape(shard, units))
        done.append(jnp.concatenate([down_part(low[1]), down_part(high[1])], 0))
        if not settled:
            settled = tuple(jnp.zeros(shape, F32) for shape in matrix_shapes)
        settled = tuple(total.at[layer].set(part) for total, part in zip(settled, done))

    packed = packed + swap_row(packed)
    other = swap_core(packed)
    narrow_sum = (packed + other)[: LAYERS * narrow].reshape(LAYERS, len(VECTORS), shard)
    unit_mine = packed[LAYERS * narrow :].reshape(LAYERS, unit_half)
    unit_other = other[LAYERS * narrow :].reshape(LAYERS, unit_half)
    summed = {name: narrow_sum[:, position] for position, name in enumerate(VECTORS)}
    summed["up_bias"] = by_core(core, unit_mine, unit_other, 1)

    query, key, value, output, up, down = settled
    final = (
        summed["first_scale"],
        summed["first_shift"],
        query,
        summed["query_bias"],
        key,
        value,
        summed["value_bias"],
        output,
        summed["output_bias"],
        summed["second_scale"],
        summed["second_shift"],
        up,
        summed["up_bias"],
        down,
        summed["down_bias"],
    )
    return (result, input_grad) + final


def solution(mesh):
    rows, vector, matrix = P("wt", "seq", None), P(None, "wt"), P(None, "wt", None)
    parameters = (
        vector,
        vector,
        matrix,
        vector,
        matrix,
        matrix,
        vector,
        matrix,
        vector,
        vector,
        vector,
        matrix,
        vector,
        matrix,
        vector,
    )
    specs = (rows, rows) + parameters
    return jax.shard_map(
        per_device, mesh=mesh, in_specs=specs, out_specs=specs, check_vma=False
    )
```

```python
import math

import jax
import jax.numpy as jnp
from jax import lax
from jax.experimental import pallas as pl
from jax.experimental.pallas import tpu as pltpu
from jax.sharding import PartitionSpec as P

HEAD_DIM = 64
LAYERS = 2
epsilon = 1e-05
BF = jnp.bfloat16
F32 = jnp.float32
VMEM_BYTES = 48 * 1024 * 1024

VECTORS = (
    "first_scale",
    "first_shift",
    "query_bias",
    "value_bias",
    "output_bias",
    "second_scale",
    "second_shift",
    "down_bias",
)
LINE_STEPS = (1, 2)


def lasting(microseconds):
    return pl.CostEstimate(
        flops=int(microseconds * 1.15e9),
        bytes_accessed=int(microseconds * 3.69e6),
        transcendentals=0,
    )


def matmul(left, right):
    return jnp.dot(left, right, preferred_element_type=F32)


def left_product(left, right):
    return lax.dot_general(left, right, (((0,), (0,)), ((), ())), preferred_element_type=F32)


def right_product(left, right):
    return lax.dot_general(left, right, (((1,), (1,)), ((), ())), preferred_element_type=F32)


def column_sums(values):
    return jnp.sum(values, axis=0, dtype=F32)


def swap_core(values):
    pairs = [(i, i ^ 1) for i in range(lax.axis_size("seq"))]
    return lax.ppermute(values, "seq", pairs)


def swap_row(values):
    pairs = [(i, i ^ 2) for i in range(lax.axis_size("seq"))]
    return lax.ppermute(values, "seq", pairs)


def by_core(core, mine, theirs, axis):
    return jnp.where(
        core == 0,
        jnp.concatenate([mine, theirs], axis),
        jnp.concatenate([theirs, mine], axis),
    )


def swap_pair(values):
    pairs = [(i, i ^ 1) for i in range(lax.axis_size("wt"))]
    return lax.ppermute(values, "wt", pairs)


def picked(values, index, axis):
    return lax.dynamic_index_in_dim(values, index, axis, keepdims=False)


def after(values, earlier):
    return lax.optimization_barrier((values, earlier))[0]


def swap_line(values, step):
    pairs = [(i, i ^ (2 * step)) for i in range(lax.axis_size("wt"))]
    return lax.ppermute(values, "wt", pairs)


def doubled(values, step):
    there = swap_line(values, step)
    return jnp.concatenate([values, there], 0), there


def place_kernel(fill, where_ref, *refs):
    fill(where_ref, *refs)


def place(fill, where, sources, spots, name):
    depth = sources[0][0].shape[0]
    rows = sources[0][0].shape[1]
    size = sum(math.prod(spot) for spot in spots) * depth

    def spot_index(spot):
        blank = (0,) * len(spot)
        return lambda k, w: (jnp.bitwise_xor(w[0], 2 * (k % 2) + k // 2),) + blank

    return pl.pallas_call(
        lambda *refs: place_kernel(fill, *refs),
        grid_spec=pltpu.PrefetchScalarGridSpec(
            num_scalar_prefetch=1,
            grid=(depth,),
            in_specs=[
                pl.BlockSpec((1, rows, width), lambda k, w, block=block: (k, 0, block))
                for _, width, block in sources
            ],
            out_specs=[pl.BlockSpec((1,) + spot, spot_index(spot)) for spot in spots],
        ),
        out_shape=[jax.ShapeDtypeStruct((depth,) + spot, BF) for spot in spots],
        compiler_params=pltpu.CompilerParams(vmem_limit_bytes=VMEM_BYTES),
        cost_estimate=lasting(3.0),
        name=name,
    )(where, *(array for array, _, _ in sources))


def piece_spots(where_ref, count):
    spots = [(0, where_ref[1]), (0, 1 - where_ref[1])]
    if count == 2:
        return spots
    return [spot + (where_ref[2],) for spot in spots] + [
        spot + (1 - where_ref[2],) for spot in spots
    ]


def fill_in(where_ref, *refs):
    sources, target = refs[:-1], refs[-1]
    for spot, source in zip(piece_spots(where_ref, len(sources)), sources):
        target[spot] = source[0]


def fill_out(where_ref, *refs):
    sources, target = refs[:-1], refs[-1]
    count = len(sources) // 2
    width = sources[0].shape[-1]
    here = pl.ds(pl.multiple_of(where_ref[3] * width, 128), width)
    there = pl.ds(pl.multiple_of((1 - where_ref[3]) * width, 128), width)
    for columns, group in ((here, sources[:count]), (there, sources[count:])):
        for spot, source in zip(piece_spots(where_ref, count), group):
            target[spot + (slice(None), columns)] = source[0]


def fill_wide(where_ref, near_ref, far_ref, near_there_ref, far_there_ref, up, down):
    rows = near_ref.shape[1] // 2
    features = down.shape[-1]
    for source, across, over in (
        (near_ref, where_ref[1], where_ref[2]),
        (far_ref, 1 - where_ref[1], where_ref[2]),
        (near_there_ref, where_ref[1], 1 - where_ref[2]),
        (far_there_ref, 1 - where_ref[1], 1 - where_ref[2]),
    ):
        up[0, across, over] = source[0, :rows]
        down[0, across, over, 0] = source[0, rows:, :features]
        down[0, across, over, 1] = source[0, rows:, features:]


class Reducer:
    def __init__(self):
        self.arrived = None
        self.stages = [None, None, None]
        self.totals = []

    def tick(self, values=None, gate=None, beside=None):
        owners = lax.axis_size("wt")
        if owners != 8:
            if values is not None:
                self.totals.append(
                    [
                        lax.psum_scatter(v, "wt", scatter_dimension=0, tiled=False).astype(F32)
                        for v in values
                    ]
                )
            return None if beside is None else swap_row(beside)
        own = lax.axis_index("wt")
        bits = (own % 2, own // 2 % 2, own // 4)
        moves = (swap_pair, lambda v: swap_line(v, 1), lambda v: swap_line(v, 2))
        axes = (1, 1, 0)
        if values is not None:
            self.stages[0] = [v.reshape((owners // 2, 2) + v.shape[1:]) for v in values]
        active = [i for i in range(3) if self.stages[i] is not None]
        sends = [[picked(v, 1 - bits[i], axes[i]) for v in self.stages[i]] for i in active]
        earlier = [v for v in (self.arrived, gate) if v is not None]
        if earlier:
            sends = [[after(v, earlier) for v in send] for send in sends]
            beside = None if beside is None else after(beside, earlier)
        theirs = [[moves[i](v) for v in send] for i, send in zip(active, sends)]
        swapped = None if beside is None else swap_row(beside)
        self.arrived = (theirs, swapped)
        following = [None, None, None]
        for i, there in zip(active, theirs):
            kept = [picked(v, bits[i], axes[i]) for v in self.stages[i]]
            total = [k.astype(F32) + t.astype(F32) for k, t in zip(kept, there)]
            if i == 2:
                self.totals.append(total)
                continue
            total = [v.astype(k.dtype) for v, k in zip(total, kept)]
            if i == 0:
                total = [v.reshape((2, 2) + v.shape[1:]) for v in total]
            following[i + 1] = total
        self.stages = following
        return swapped

    def finish(self):
        while any(stage is not None for stage in self.stages):
            self.tick()


def attend_kernel(q_ref, k_ref, v_ref, o_ref):
    factor = 1.0 / math.sqrt(HEAD_DIM)
    for head in range(q_ref.shape[1] // HEAD_DIM):
        part = slice(head * HEAD_DIM, (head + 1) * HEAD_DIM)
        scores = right_product(q_ref[:, part], k_ref[:, part]) * factor
        raised = jnp.exp(scores - jnp.max(scores, axis=1, keepdims=True))
        chances = raised * (1.0 / jnp.sum(raised, axis=1, keepdims=True))
        o_ref[:, part] = matmul(chances.astype(BF), v_ref[:, part]).astype(BF)


def attend(qkv):
    rows, width = qkv.shape
    width //= 3
    block = 2 * HEAD_DIM
    steps = width // block
    return pl.pallas_call(
        attend_kernel,
        grid=(steps,),
        in_specs=[
            pl.BlockSpec((rows, block), lambda i: (0, i)),
            pl.BlockSpec((rows, block), lambda i: (0, steps + i)),
            pl.BlockSpec((rows, block), lambda i: (0, 2 * steps + i)),
        ],
        out_specs=pl.BlockSpec((rows, block), lambda i: (0, i)),
        out_shape=jax.ShapeDtypeStruct((rows, width), BF),
        compiler_params=pltpu.CompilerParams(vmem_limit_bytes=VMEM_BYTES),
        cost_estimate=lasting(6.0),
        name="attend",
    )(qkv, qkv, qkv)


def attend_back_kernel(q_ref, k_ref, v_ref, eo_ref, eq_ref, ek_ref, ev_ref):
    factor = 1.0 / math.sqrt(HEAD_DIM)
    for head in range(q_ref.shape[1] // HEAD_DIM):
        part = slice(head * HEAD_DIM, (head + 1) * HEAD_DIM)
        queries, keys, eo = q_ref[:, part], k_ref[:, part], eo_ref[:, part]
        scores = right_product(keys, queries) * factor
        raised = jnp.exp(scores - jnp.max(scores, axis=0, keepdims=True))
        chances = raised * (1.0 / jnp.sum(raised, axis=0, keepdims=True))
        ep = right_product(v_ref[:, part], eo)
        ev_ref[:, part] = matmul(chances.astype(BF), eo).astype(BF)
        inner = jnp.sum(ep * chances, axis=0, keepdims=True)
        es = (chances * (ep - inner)).astype(BF)
        ek_ref[:, part] = (matmul(es, queries) * factor).astype(BF)
        eq_ref[:, part] = (left_product(keys, es) * factor).T.astype(BF)


def attend_back(qkv, eo):
    rows, width = eo.shape
    block = 2 * HEAD_DIM
    steps = width // block
    return pl.pallas_call(
        attend_back_kernel,
        grid=(steps,),
        in_specs=[
            pl.BlockSpec((rows, block), lambda i: (0, i)),
            pl.BlockSpec((rows, block), lambda i: (0, steps + i)),
            pl.BlockSpec((rows, block), lambda i: (0, 2 * steps + i)),
            pl.BlockSpec((rows, block), lambda i: (0, i)),
        ],
        out_specs=[pl.BlockSpec((rows, block), lambda i: (0, i))] * 3,
        out_shape=[jax.ShapeDtypeStruct((rows, width), BF)] * 3,
        compiler_params=pltpu.CompilerParams(vmem_limit_bytes=VMEM_BYTES),
        cost_estimate=lasting(8.2),
        name="attend_back",
    )(qkv, qkv, qkv, eo)


def norm_parts(values):
    centred = values - jnp.mean(values, axis=-1, keepdims=True)
    spread = jnp.mean(centred * centred, axis=-1, keepdims=True)
    rate = lax.rsqrt(spread + epsilon)
    return centred * rate, rate


def pack_kernel(where_ref, *refs):
    *squares, up_ref, down_ref, branch_ref, wide_ref = refs
    side, core = where_ref[2], where_ref[3]
    shard, features = squares[0].shape[1:]
    half, part = features // 2, shard // 2
    unit_half = down_ref.shape[1] // 2
    columns = pl.ds(pl.multiple_of(core * half, 128), half)
    for position, square in enumerate(squares):
        branch_ref[:, position * half : (position + 1) * half] = square[0, :, columns]
    rows = up_ref[0, pl.ds(pl.multiple_of(side * part, 16), part), :]
    chosen = []
    for owner in range(up_ref.shape[2] // (2 * unit_half)):
        first = 2 * owner * unit_half
        low = rows[:, first : first + unit_half]
        high = rows[:, first + unit_half : first + 2 * unit_half]
        chosen.append(jnp.where(core == 0, low, high))
    wide_ref[:part, :] = jnp.concatenate(chosen, 1)
    for pair in range(2):
        first = pl.multiple_of(core * unit_half + side * shard, 16) + pair * part
        wide_ref[part:, pair * features : (pair + 1) * features] = down_ref[
            0, pl.ds(first, part), :
        ]


def pack(where, squares, up, down, layer):
    members = (*squares, up, down)
    shard, features = squares[0].shape[1:]
    shape = (shard, 2 * features)
    return pl.pallas_call(
        pack_kernel,
        grid=(1,),
        in_specs=[pl.BlockSpec(memory_space=pltpu.SMEM)]
        + [pl.BlockSpec((1,) + v.shape[1:], lambda i: (layer, 0, 0)) for v in members],
        out_specs=[pl.BlockSpec(shape, lambda i: (0, 0))] * 2,
        out_shape=[jax.ShapeDtypeStruct(shape, BF)] * 2,
        compiler_params=pltpu.CompilerParams(vmem_limit_bytes=60 * 1024 * 1024),
        cost_estimate=lasting(3.0),
        name="pack",
    )(where, *members)


def norm_next_kernel(base_ref, partial_ref, *refs):
    *theirs, bias_ref, scale_ref, shift_ref, value_ref, normed_ref = refs
    value = base_ref[...] + partial_ref[...] + bias_ref[...]
    for there in theirs:
        value = value + there[...].astype(F32)
    value_ref[...] = value
    flat, _ = norm_parts(value)
    normed_ref[...] = (flat * scale_ref[...] + shift_ref[...]).astype(BF)


def norm_next(base, parts, bias, scale, shift):
    rows, features = base.shape
    block = pl.BlockSpec((rows // 4, features), lambda i: (i, 0))
    line = pl.BlockSpec((1, features), lambda i: (0, 0))
    return pl.pallas_call(
        norm_next_kernel,
        grid=(4,),
        in_specs=[block] * (1 + len(parts)) + [line] * 3,
        out_specs=[block] * 2,
        out_shape=[
            jax.ShapeDtypeStruct((rows, features), F32),
            jax.ShapeDtypeStruct((rows, features), BF),
        ],
        compiler_params=pltpu.CompilerParams(vmem_limit_bytes=VMEM_BYTES),
        cost_estimate=lasting(2.9),
        name="norm_next",
    )(base, *parts, *(v.reshape(1, features) for v in (bias, scale, shift)))


def norm_back_kernel(offset_ref, partial_ref, there_ref, value_ref, scale_ref, base_ref, *outs):
    out_ref, low_ref, sums_ref = outs

    @pl.when(pl.program_id(0) == 0)
    def _():
        sums_ref[...] = jnp.zeros_like(sums_ref)

    grad = partial_ref[...] + there_ref[...].astype(F32)
    flat, rate = norm_parts(value_ref[...])
    inner = grad * scale_ref[...]
    mean_inner = jnp.mean(inner, axis=-1, keepdims=True)
    mean_cross = jnp.mean(inner * flat, axis=-1, keepdims=True)
    total = base_ref[...] + rate * (inner - mean_inner - flat * mean_cross)
    out_ref[...] = total
    low = total.astype(BF)
    low_ref[...] = low
    sums_ref[0:1] += jnp.sum(grad * flat, axis=0, keepdims=True)
    sums_ref[1:2] += jnp.sum(grad, axis=0, keepdims=True)
    sums_ref[2:3] += jnp.sum(low.astype(F32), axis=0, keepdims=True)


def norm_back(partial, there, value, scale, base, offset):
    rows, features = there.shape
    block = rows // 4
    steps = rows // block
    moved = pl.BlockSpec((block, features), lambda i, w: (w[0] * steps + i, 0))
    plain = pl.BlockSpec((block, features), lambda i, w: (i, 0))
    return pl.pallas_call(
        norm_back_kernel,
        grid_spec=pltpu.PrefetchScalarGridSpec(
            num_scalar_prefetch=1,
            grid=(steps,),
            in_specs=[
                moved,
                plain,
                moved,
                pl.BlockSpec((1, features), lambda i, w: (0, 0)),
                moved,
            ],
            out_specs=[plain, plain, pl.BlockSpec((8, features), lambda i, w: (0, 0))],
        ),
        out_shape=[
            jax.ShapeDtypeStruct((rows, features), F32),
            jax.ShapeDtypeStruct((rows, features), BF),
            jax.ShapeDtypeStruct((8, features), F32),
        ],
        compiler_params=pltpu.CompilerParams(vmem_limit_bytes=VMEM_BYTES),
        cost_estimate=lasting(3.8),
        name="norm_back",
    )(offset, partial, there, value, scale.reshape(1, features), base)


def gelu_parts(values):
    below = 0.5 * (1.0 + lax.erf(values * math.sqrt(0.5)))
    density = jnp.exp(-0.5 * values * values) * (1.0 / math.sqrt(2.0 * math.pi))
    return values * below, below + values * density


def settle_kernel(where_ref, *refs):
    *squares, up, down = refs[-6:]
    side, core = where_ref[2], where_ref[3]
    shard, features = squares[0].shape[1:]
    half, part = features // 2, shard // 2
    unit_half = down.shape[1] // 2
    owners = up.shape[2] // (2 * unit_half)
    pieces = 3 if refs[1].shape[0] == shard else 2
    mine_ref, *mine_wide = refs[:pieces]
    other_ref, *other_wide = refs[pieces : 2 * pieces]
    here = pl.ds(pl.multiple_of(core * half, 128), half)
    there = pl.ds(pl.multiple_of((1 - core) * half, 128), half)
    for position, target in enumerate(squares):
        columns = slice(position * half, (position + 1) * half)
        target[0, :, here] = mine_ref[:, columns].astype(F32)
        target[0, :, there] = other_ref[:, columns].astype(F32)
    spread = [0] if pieces == 2 else [side, 1 - side]
    rows = shard if pieces == 2 else part
    for where, mine_part, other_part in zip(spread, mine_wide, other_wide):
        mine, other = mine_part[:rows].astype(F32), other_part[:rows].astype(F32)
        low = jnp.where(core == 0, mine, other)
        high = jnp.where(core == 0, other, mine)
        target = pl.ds(where * rows if pieces == 2 else pl.multiple_of(where * rows, 8), rows)
        for owner in range(owners):
            columns = slice(owner * unit_half, (owner + 1) * unit_half)
            up[0, target, 2 * owner * unit_half : 2 * (owner + 1) * unit_half] = jnp.concatenate(
                [low[:, columns], high[:, columns]], 1
            )
        for pair in range(2):
            columns = slice(pair * features, (pair + 1) * features)
            for source, place_core in ((mine_part, core), (other_part, 1 - core)):
                first = place_core * unit_half + where * shard
                target = pl.ds(pl.multiple_of(first, 8) + pair * rows, rows)
                down[0, target] = source[rows:, columns].astype(F32)


def settle(core, pieces, earlier, layer, shapes):
    size = sum(math.prod(shape[1:]) for shape in shapes)
    return pl.pallas_call(
        settle_kernel,
        grid=(1,),
        in_specs=[pl.BlockSpec(memory_space=pltpu.SMEM)]
        + [pl.BlockSpec(piece.shape, lambda i: (0, 0)) for piece in pieces]
        + [pl.BlockSpec(memory_space=pl.ANY)] * len(earlier),
        out_specs=[
            pl.BlockSpec((1,) + shape[1:], lambda i: (layer, 0, 0)) for shape in shapes
        ],
        out_shape=[jax.ShapeDtypeStruct(shape, F32) for shape in shapes],
        input_output_aliases={1 + len(pieces) + i: i for i in range(len(earlier))},
        compiler_params=pltpu.CompilerParams(vmem_limit_bytes=VMEM_BYTES),
        cost_estimate=lasting(2.0),
        name="settle",
    )(core, *pieces, *earlier)


def per_device(
    activations,
    upstream,
    first_scale,
    first_shift,
    query_weight,
    query_bias,
    key_weight,
    value_weight,
    value_bias,
    output_weight,
    output_bias,
    second_scale,
    second_shift,
    up_weight,
    up_bias,
    down_weight,
    down_bias,
):
    owners = lax.axis_size("wt")
    seat = lax.axis_index("seq")
    core, side = seat % 2, seat // 2
    frames_here, features = activations.shape[1:]
    half = features // 2
    shard = features // owners
    units = up_weight.shape[2]
    unit_shard = units // owners
    unit_half = unit_shard // 2

    def to_chip(values):
        kept = lax.dynamic_index_in_dim(values, side, 0, keepdims=False)
        sent = lax.dynamic_index_in_dim(values, 1 - side, 0, keepdims=False)
        mine = jnp.concatenate([kept, swap_row(sent)], 0)
        return by_core(core, mine, swap_core(mine), 0)

    def from_chip(mine, other):
        kept = mine[:frames_here]
        return jnp.where(side == 0, jnp.stack([kept, other]), jnp.stack([other, kept]))

    def by_side(mine, there):
        low, high = jnp.where(side == 0, mine, there), jnp.where(side == 0, there, mine)
        part = shard // 2
        low_down, high_down = low[part:], high[part:]
        return jnp.concatenate(
            [
                low[:part],
                high[:part],
                jnp.concatenate([low_down[:, :features], high_down[:, :features]], 1),
                jnp.concatenate([low_down[:, features:], high_down[:, features:]], 1),
            ],
            0,
        )

    def own_rows(values):
        return lax.dynamic_slice_in_dim(values, core * 2 * frames_here, 2 * frames_here, 0)

    def half_columns(values):
        return lax.dynamic_slice_in_dim(values, core * half, half, 1)

    direct = owners == 8
    own = lax.axis_index("wt")
    line, across = own // 2, own % 2
    where = jnp.stack([line, across, side, core]).astype(jnp.int32)

    down_in = to_chip(upstream)
    shards = {}
    for layer in range(LAYERS):
        shards["branch", layer] = jnp.concatenate(
            [
                half_columns(query_weight[layer]),
                half_columns(key_weight[layer]),
                half_columns(value_weight[layer]),
                half_columns(output_weight[layer]),
            ],
            1,
        )
    for layer in range(LAYERS):
        shards["up", layer] = picked(
            up_weight[layer].reshape(shard, owners, 2, unit_half), core, 2
        ).reshape(shard, units // 2)
        shards["down", layer] = lax.dynamic_slice_in_dim(
            down_weight[layer], core * unit_half, unit_half, 0
        )
    members = dict(
        first_scale=first_scale,
        first_shift=first_shift,
        query_bias=query_bias,
        value_bias=value_bias,
        output_bias=output_bias,
        second_scale=second_scale,
        second_shift=second_shift,
        down_bias=down_bias,
    )
    narrow = len(VECTORS) * shard
    packed = jnp.concatenate([members[name] for name in VECTORS] + [up_bias], 1)
    gathered = {}
    if direct:

        squares = (query_weight, key_weight, value_weight, output_weight)
        branch_piece, wide_piece = zip(
            *(pack(where, squares, up_weight, down_weight, layer) for layer in range(LAYERS))
        )

        wide, branch = [None, None], [None, None]
        wide_far, branch_far = [None, None], [None, None]
        wide_there, wide_far_there = [None, None], [None, None]
        wide_hop, first = doubled(wide_piece[0][None], 2)

        wide[0], tied = doubled(after(wide_hop, first), 1)
        branch_hop, also = doubled(after(branch_piece[0][None], first), 2)
        packed_hop, _ = doubled(after(packed[None], first), 2)
        earlier = (tied, also, down_in)

        wide_far[0] = swap_pair(after(wide[0], earlier))
        wide_there[0] = swap_row(after(wide[0], earlier))
        branch[0], tied = doubled(after(branch_hop, earlier), 1)
        wide_hop, also = doubled(after(wide_piece[1][None], earlier), 2)
        packed_line, _ = doubled(after(packed_hop, earlier), 1)
        earlier = (tied, also, wide_far[0], wide_there[0])

        branch_far[0] = swap_pair(after(branch[0], earlier))
        wide_far_there[0] = swap_row(after(wide_far[0], earlier))
        wide[1], tied = doubled(after(wide_hop, earlier), 1)
        branch_hop, also = doubled(after(branch_piece[1][None], earlier), 2)
        packed_far = swap_pair(after(packed_line, earlier))
        earlier = (tied, also, branch_far[0], wide_far_there[0])

        wide_far[1] = swap_pair(after(wide[1], earlier))
        wide_there[1] = swap_row(after(wide[1], earlier))
        branch[1], tied = doubled(after(branch_hop, earlier), 1)
        third = (wide_far[1], wide_there[1], tied)

        branch_far[1], wide_far_there[1] = lax.optimization_barrier(
            (swap_pair(after(branch[1], third)), swap_row(after(wide_far[1], third)))
        )

        for layer in range(LAYERS):
            pieces = (branch[layer], branch_far[layer])
            (gathered["in", layer],) = place(
                fill_in,
                where,
                tuple((v, 3 * half, 0) for v in pieces),
                ((2, shard, 3 * half),),
                "place_in",
            )
            gathered["in", layer] = gathered["in", layer].reshape(features, 3 * half)
            swapped = swap_core(jnp.concatenate([v[:, :, 3 * half :] for v in pieces], 2))
            (gathered["out", layer],) = place(
                fill_out,
                where,
                tuple((v, half, 3) for v in pieces) + ((swapped, half, 0), (swapped, half, 1)),
                ((2, shard, features),),
                "place_out",
            )
            gathered["out", layer] = gathered["out", layer].reshape(features, features)
            width = 2 * features
            pieces = (wide[layer], wide_far[layer], wide_there[layer], wide_far_there[layer])
            gathered["up", layer], gathered["down", layer] = place(
                fill_wide,
                where,
                tuple((v, width, 0) for v in pieces),
                ((2, 2, shard // 2, width), (2, 2, 2, shard // 2, features)),
                "place_wide",
            )
            gathered["up", layer] = gathered["up", layer].reshape(features, units // 2)
            gathered["down", layer] = gathered["down", layer].reshape(units // 2, features)
    else:
        for layer in range(LAYERS):
            for kind in ("up", "down"):
                gathered[kind, layer] = lax.all_gather(
                    shards[kind, layer], "wt", axis=0, tiled=True
                )
            branch = lax.all_gather(shards["branch", layer], "wt", axis=0, tiled=True)
            gathered["in", layer] = branch[:, : 3 * half]
            out_half = branch[:, 3 * half :]
            gathered["out", layer] = by_core(core, out_half, swap_core(out_half), 1)
    if direct:
        spread = jnp.stack([packed_line, packed_far], 1)
        spread = spread.reshape((2, 2, 2) + packed.shape).swapaxes(0, 1)
        spread = spread.reshape((owners // 2, 2) + packed.shape)
        for bit in LINE_STEPS:
            turned = spread.reshape((owners // (4 * bit), 2, bit, 2) + packed.shape)
            spread = jnp.where((line & bit) == 0, turned, turned[:, ::-1]).reshape(spread.shape)
        spread = jnp.where(across == 0, spread, spread[:, ::-1]).reshape(
            (owners,) + packed.shape
        )
    else:
        spread = lax.all_gather(packed, "wt", axis=0, tiled=False)
    vector_rows = (
        spread[:, :, :narrow]
        .reshape(owners, LAYERS * len(VECTORS), shard)
        .swapaxes(0, 1)
        .reshape(LAYERS * len(VECTORS), features)
        .astype(F32)
    )
    vectors = [
        {
            name: vector_rows[layer * len(VECTORS) + position]
            for position, name in enumerate(VECTORS)
        }
        for layer in range(LAYERS)
    ]
    unit_rows = (
        picked(spread[:, :, narrow:].reshape(owners, LAYERS, 2, unit_half), core, 2)
        .swapaxes(0, 1)
        .reshape(LAYERS, units // 2)
        .astype(F32)
    )

    weights = [
        tuple(gathered[kind, layer] for kind in ("in", "out", "up", "down"))
        for layer in range(LAYERS)
    ]

    hidden = to_chip(activations).astype(F32)
    kept = []
    for layer in range(LAYERS):
        vec = vectors[layer]
        in_weight, out_weight, up, down = weights[layer]
        if layer == 0:
            flat, _ = norm_parts(hidden)
            normed = (flat * vec["first_scale"] + vec["first_shift"]).astype(BF)
        in_bias = jnp.concatenate(
            [
                lax.dynamic_slice_in_dim(vec["query_bias"], core * half, half, 0),
                jnp.zeros((half,), F32),
                lax.dynamic_slice_in_dim(vec["value_bias"], core * half, half, 0),
            ]
        )
        qkv = (matmul(normed, in_weight) + in_bias).astype(BF)
        mixture_half = attend(qkv)
        mixture = by_core(core, mixture_half, swap_core(mixture_half), 1)
        middle, second = norm_next(
            hidden,
            (matmul(mixture, out_weight),),
            vec["output_bias"],
            vec["second_scale"],
            vec["second_shift"],
        )
        upward = matmul(second, up) + unit_rows[layer]
        activated, slope = gelu_parts(upward)
        activated = activated.astype(BF)
        if direct and layer == 0:
            activated = after(activated, third)
        slope = slope.astype(BF)
        kept.append((hidden, normed, qkv, mixture, middle, second, activated, slope))
        partial = matmul(activated, down)
        if layer + 1 < LAYERS:
            hidden, normed = norm_next(
                middle,
                (partial, swap_core(partial.astype(BF))),
                vec["down_bias"],
                vectors[layer + 1]["first_scale"],
                vectors[layer + 1]["first_shift"],
            )
        else:
            theirs = lax.dynamic_slice_in_dim(
                partial, (1 - core) * 2 * frames_here, 2 * frames_here, 0
            )
            total = own_rows(partial) + swap_core(theirs.astype(BF))
            result_rows = (own_rows(middle) + vec["down_bias"] + total).astype(BF)

    grad_hidden = down_in.astype(F32)
    grad_down_bias = column_sums(down_in)[None]
    vector_grads = [None] * LAYERS
    settled = ()
    reducer = Reducer()
    row_core = core.reshape(1).astype(jnp.int32)
    no_offset = jnp.zeros((1,), jnp.int32)
    matrix_shapes = tuple(
        (LAYERS,) + shape
        for shape in ((shard, features),) * 4 + ((shard, units), (unit_shard, features))
    )
    for layer in reversed(range(LAYERS)):
        vec = vectors[layer]
        in_weight, out_weight, up, down = weights[layer]
        hidden, normed, qkv, mixture, middle, second, activated, slope = kept[layer]
        grad_down = left_product(activated, down_in).astype(BF)
        grad_upward = (slope.astype(F32) * right_product(down_in, down)).astype(BF)
        grad_up = left_product(second, grad_upward).astype(BF)
        if layer > 0:
            grad_up = grad_up.reshape(owners, shard, units // 2)
            reducer.tick([grad_down.reshape(owners, unit_half, features)])
        else:
            grad_up = grad_up.reshape(owners, 2, shard // 2, units // 2)
            grad_down = grad_down.reshape(owners, 2, 2, shard // 2, features)
            grad_down = jnp.concatenate([grad_down[:, :, 0], grad_down[:, :, 1]], -1)
            down_there = reducer.tick([grad_branch], beside=picked(grad_down, 1 - side, 1))
        grad_up_bias = column_sums(grad_upward)
        partial = right_product(grad_upward, up)
        there = swap_core(partial.astype(BF))
        grad_middle, branch_in, second_sums = norm_back(
            partial, there, middle, vec["second_scale"], grad_hidden, no_offset
        )
        grad_out = left_product(mixture, half_columns(branch_in))
        out_rows = lax.dynamic_slice_in_dim(out_weight, core * half, half, 0)
        grad_mixture = right_product(branch_in, out_rows).astype(BF)
        grad_qkv = jnp.concatenate(attend_back(qkv, grad_mixture), 1)
        grad_in = left_product(normed, grad_qkv).astype(BF)
        grad_branch = jnp.concatenate([grad_in, grad_out.astype(BF)], 1)
        grad_branch = grad_branch.reshape(owners, shard, 2 * features)
        if layer > 0:
            result_there = reducer.tick(
                [grad_up], grad_branch, beside=result_rows[frames_here:]
            )
        else:
            up_there = reducer.tick([grad_branch], beside=picked(grad_up, 1 - side, 1))
            grad_wide = jnp.concatenate(
                [
                    (picked(grad_up, side, 1).astype(F32) + up_there.astype(F32)).astype(BF),
                    (picked(grad_down, side, 1).astype(F32) + down_there.astype(F32)).astype(BF),
                ],
                1,
            )
        grad_in_bias = column_sums(grad_qkv)
        partial = right_product(grad_qkv, in_weight)
        below = grad_down_bias
        if layer > 0:
            there = swap_core(partial.astype(BF))
            grad_hidden, down_in, first_sums = norm_back(
                partial, there, hidden, vec["first_scale"], grad_middle, no_offset
            )
            grad_down_bias = first_sums[2:3]
        else:
            theirs = lax.dynamic_slice_in_dim(
                partial, (1 - core) * 2 * frames_here, 2 * frames_here, 0
            )
            there = swap_core(theirs.astype(BF))
            before, _, first_sums = norm_back(
                partial, there, hidden, vec["first_scale"], grad_middle, row_core
            )

        twice = jnp.stack([grad_in_bias[:half], grad_in_bias[2 * half :]])
        rows = jnp.concatenate(
            [
                first_sums[:2],
                jnp.concatenate([twice, twice], 1),
                second_sums[2:3],
                second_sums[:2],
                below,
            ],
            0,
        )
        place_row = lax.broadcasted_iota(jnp.int32, rows.shape, 0)
        on_right = lax.broadcasted_iota(jnp.int32, rows.shape, 1) >= half
        counted = jnp.where((place_row == 2) | (place_row == 3), on_right == (core == 1), core == 0)
        if layer == 0:
            counted = counted | (place_row < 2)
        vector_grads[layer] = (jnp.where(counted, rows, 0.0), grad_up_bias)

    packed = jnp.stack([rows for rows, _ in vector_grads])
    packed = packed.reshape(LAYERS * len(VECTORS), owners, shard).swapaxes(0, 1)
    packed = packed.reshape(owners, LAYERS * narrow)
    from_units = jnp.stack([values for _, values in vector_grads])
    from_units = from_units.reshape(LAYERS, owners, unit_half).swapaxes(0, 1)
    from_units = from_units.reshape(owners, LAYERS * unit_half)
    packed = jnp.concatenate([packed, from_units], 1)
    before = after(before, (reducer.arrived, packed))
    reducer.tick([grad_wide, packed])
    result = from_chip(result_rows, result_there)
    input_grad = from_chip(before, swap_row(before[frames_here:]))
    reducer.finish()
    for layer in reversed(range(LAYERS)):
        if layer > 0:
            (grad_down,), (grad_up,), (grad_branch,) = reducer.totals[:3]
            grad_wide = jnp.concatenate(
                [grad_up, jnp.concatenate([grad_down[:shard], grad_down[shard:]], 1)], 0
            )
        else:
            (grad_branch,), (grad_wide, packed) = reducer.totals[3:]

        def over_sides(values):
            values = values.astype(BF)
            there = swap_row(values)
            if layer > 0:
                there = after(there, reducer.arrived)
            values = (values.astype(F32) + there.astype(F32)).astype(BF)
            return values, swap_core(values)

        if layer > 0:
            mine, other = over_sides(jnp.concatenate([grad_branch, grad_wide], 0))
            mine, other = (mine[:shard], mine[shard:]), (other[:shard], other[shard:])
        else:
            mine, other = over_sides(grad_branch)
            wide_mine = grad_wide.astype(BF)
            wide_there = after(swap_row(wide_mine), settled)
            mine = (mine, wide_mine, wide_there)
            other = (other, swap_core(wide_mine), swap_core(wide_there))
        if direct:
            settled = settle(where, mine + other, settled, layer, matrix_shapes)
            continue
        if layer == 0:
            mine, other = (mine[0], by_side(*mine[1:])), (other[0], by_side(*other[1:]))
        low = [jnp.where(core == 0, m, o).astype(F32) for m, o in zip(mine, other)]
        high = [jnp.where(core == 0, o, m).astype(F32) for m, o in zip(mine, other)]
        done = []
        for position in range(4):
            part = slice(position * half, (position + 1) * half)
            done.append(jnp.concatenate([low[0][:, part], high[0][:, part]], 1))

        def up_part(values):
            return values[:shard].reshape(shard, owners, unit_half)

        def down_part(values):
            return jnp.concatenate([values[shard:, :features], values[shard:, features:]], 0)

        done.append(jnp.stack([up_part(low[1]), up_part(high[1])], 2).reshape(shard, units))
        done.append(jnp.concatenate([down_part(low[1]), down_part(high[1])], 0))
        if not settled:
            settled = tuple(jnp.zeros(shape, F32) for shape in matrix_shapes)
        settled = tuple(total.at[layer].set(part) for total, part in zip(settled, done))

    packed = packed + swap_row(packed)
    other = swap_core(packed)
    narrow_sum = (packed + other)[: LAYERS * narrow].reshape(LAYERS, len(VECTORS), shard)
    unit_mine = packed[LAYERS * narrow :].reshape(LAYERS, unit_half)
    unit_other = other[LAYERS * narrow :].reshape(LAYERS, unit_half)
    summed = {name: narrow_sum[:, position] for position, name in enumerate(VECTORS)}
    summed["up_bias"] = by_core(core, unit_mine, unit_other, 1)

    query, key, value, output, up, down = settled
    final = (
        summed["first_scale"],
        summed["first_shift"],
        query,
        summed["query_bias"],
        key,
        value,
        summed["value_bias"],
        output,
        summed["output_bias"],
        summed["second_scale"],
        summed["second_shift"],
        up,
        summed["up_bias"],
        down,
        summed["down_bias"],
    )
    return (result, input_grad) + final


def solution(mesh):
    rows, vector, matrix = P("wt", "seq", None), P(None, "wt"), P(None, "wt", None)
    parameters = (
        vector,
        vector,
        matrix,
        vector,
        matrix,
        matrix,
        vector,
        matrix,
        vector,
        vector,
        vector,
        matrix,
        vector,
        matrix,
        vector,
    )
    specs = (rows, rows) + parameters
    return jax.shard_map(
        per_device, mesh=mesh, in_specs=specs, out_specs=specs, check_vma=False
    )
```

```python
import math

import jax
import jax.numpy as jnp
from jax import lax
from jax.experimental import pallas as pl
from jax.experimental.pallas import tpu as pltpu
from jax.sharding import PartitionSpec as P

HEAD_DIM = 64
LAYERS = 2
epsilon = 1e-05
BF = jnp.bfloat16
F32 = jnp.float32
VMEM_BYTES = 32 * 1024 * 1024

VECTORS = (
    "first_scale",
    "first_shift",
    "query_bias",
    "value_bias",
    "output_bias",
    "second_scale",
    "second_shift",
    "down_bias",
)
LINE_STEPS = (1, 2)


def lasting(microseconds):
    return pl.CostEstimate(
        flops=int(microseconds * 1.15e9),
        bytes_accessed=int(microseconds * 3.69e6),
        transcendentals=0,
    )


def matmul(left, right):
    return jnp.dot(left, right, preferred_element_type=F32)


def left_product(left, right):
    return lax.dot_general(left, right, (((0,), (0,)), ((), ())), preferred_element_type=F32)


def right_product(left, right):
    return lax.dot_general(left, right, (((1,), (1,)), ((), ())), preferred_element_type=F32)


def column_sums(values):
    return jnp.sum(values, axis=0, dtype=F32)


def swap_core(values):
    pairs = [(i, i ^ 1) for i in range(lax.axis_size("seq"))]
    return lax.ppermute(values, "seq", pairs)


def swap_row(values):
    pairs = [(i, i ^ 2) for i in range(lax.axis_size("seq"))]
    return lax.ppermute(values, "seq", pairs)


def by_core(core, mine, theirs, axis):
    return jnp.where(
        core == 0,
        jnp.concatenate([mine, theirs], axis),
        jnp.concatenate([theirs, mine], axis),
    )


def swap_pair(values):
    pairs = [(i, i ^ 1) for i in range(lax.axis_size("wt"))]
    return lax.ppermute(values, "wt", pairs)


def picked(values, index, axis):
    return lax.dynamic_index_in_dim(values, index, axis, keepdims=False)


def after(values, earlier):
    return lax.optimization_barrier((values, earlier))[0]


def swap_line(values, step):
    pairs = [(i, i ^ (2 * step)) for i in range(lax.axis_size("wt"))]
    return lax.ppermute(values, "wt", pairs)


def doubled(values, step):
    there = swap_line(values, step)
    return jnp.concatenate([values, there], 0), there


def place_kernel(fill, where_ref, *refs):
    fill(where_ref, *refs)


def last_kernel(where_ref, source_ref, *refs):
    up, down = refs[-2:]
    rows = source_ref.shape[1] // 2
    features = down.shape[-1]
    up[0, 0, 0] = source_ref[0, :rows]
    down[0, 0, 0, 0] = source_ref[0, rows:, :features]
    down[0, 0, 0, 1] = source_ref[0, rows:, features:]


def place_last(where, source, earlier):
    depth, rows, width = source.shape

    def spot_index(w, k, blank):
        line = jnp.bitwise_xor(w[0], 2 * (k % 2) + k // 2)
        return (line, 1 - w[1], 1 - w[2]) + (0,) * blank

    return pl.pallas_call(
        last_kernel,
        grid_spec=pltpu.PrefetchScalarGridSpec(
            num_scalar_prefetch=1,
            grid=(depth,),
            in_specs=[pl.BlockSpec((1, rows, width), lambda k, w: (k, 0, 0))]
            + [pl.BlockSpec(memory_space=pl.ANY)] * 2,
            out_specs=[
                pl.BlockSpec((1, 1, 1) + v.shape[3:], lambda k, w, n=v.ndim: spot_index(w, k, n - 3))
                for v in earlier
            ],
        ),
        out_shape=[jax.ShapeDtypeStruct(v.shape, BF) for v in earlier],
        input_output_aliases={2: 0, 3: 1},
        compiler_params=pltpu.CompilerParams(vmem_limit_bytes=VMEM_BYTES),
        cost_estimate=lasting(1.5),
        name="place_last",
    )(where, source, *earlier)


def place(fill, where, sources, spots, name):
    depth = sources[0][0].shape[0]
    rows = sources[0][0].shape[1]
    size = sum(math.prod(spot) for spot in spots) * depth

    def spot_index(spot):
        blank = (0,) * len(spot)
        return lambda k, w: (jnp.bitwise_xor(w[0], 2 * (k % 2) + k // 2),) + blank

    return pl.pallas_call(
        lambda *refs: place_kernel(fill, *refs),
        grid_spec=pltpu.PrefetchScalarGridSpec(
            num_scalar_prefetch=1,
            grid=(depth,),
            in_specs=[
                pl.BlockSpec((1, rows, width), lambda k, w, block=block: (k, 0, block))
                for _, width, block in sources
            ],
            out_specs=[pl.BlockSpec((1,) + spot, spot_index(spot)) for spot in spots],
        ),
        out_shape=[jax.ShapeDtypeStruct((depth,) + spot, BF) for spot in spots],
        compiler_params=pltpu.CompilerParams(vmem_limit_bytes=VMEM_BYTES),
        cost_estimate=lasting(3.0),
        name=name,
    )(where, *(array for array, _, _ in sources))


def piece_spots(where_ref, count):
    spots = [(0, where_ref[1]), (0, 1 - where_ref[1])]
    if count == 2:
        return spots
    return [spot + (where_ref[2],) for spot in spots] + [
        spot + (1 - where_ref[2],) for spot in spots
    ]


def fill_in(where_ref, *refs):
    sources, target = refs[:-1], refs[-1]
    for spot, source in zip(piece_spots(where_ref, len(sources)), sources):
        target[spot] = source[0]


def fill_out(where_ref, *refs):
    sources, target = refs[:-1], refs[-1]
    count = len(sources) // 2
    width = sources[0].shape[-1]
    here = pl.ds(pl.multiple_of(where_ref[3] * width, 128), width)
    there = pl.ds(pl.multiple_of((1 - where_ref[3]) * width, 128), width)
    for columns, group in ((here, sources[:count]), (there, sources[count:])):
        for spot, source in zip(piece_spots(where_ref, count), group):
            target[spot + (slice(None), columns)] = source[0]


def fill_wide(where_ref, near_ref, far_ref, near_there_ref, up, down):
    rows = near_ref.shape[1] // 2
    features = down.shape[-1]
    for source, across, over in (
        (near_ref, where_ref[1], where_ref[2]),
        (far_ref, 1 - where_ref[1], where_ref[2]),
        (near_there_ref, where_ref[1], 1 - where_ref[2]),
    ):
        up[0, across, over] = source[0, :rows]
        down[0, across, over, 0] = source[0, rows:, :features]
        down[0, across, over, 1] = source[0, rows:, features:]


class Reducer:
    def __init__(self):
        self.arrived = None
        self.stages = [None, None, None]
        self.totals = []

    def tick(self, values=None, gate=None, beside=None):
        owners = lax.axis_size("wt")
        if owners != 8:
            if values is not None:
                self.totals.append(
                    [
                        lax.psum_scatter(v, "wt", scatter_dimension=0, tiled=False).astype(F32)
                        for v in values
                    ]
                )
            return None if beside is None else jax.tree.map(swap_row, beside)
        own = lax.axis_index("wt")
        bits = (own % 2, own // 2 % 2, own // 4)
        moves = (swap_pair, lambda v: swap_line(v, 1), lambda v: swap_line(v, 2))
        axes = (1, 1, 0)
        if values is not None:
            self.stages[0] = [v.reshape((owners // 2, 2) + v.shape[1:]) for v in values]
        active = [i for i in range(3) if self.stages[i] is not None]
        sends = [[picked(v, 1 - bits[i], axes[i]) for v in self.stages[i]] for i in active]
        earlier = [v for v in (self.arrived, gate) if v is not None]
        if earlier:
            sends = [[after(v, earlier) for v in send] for send in sends]
            beside = None if beside is None else after(beside, earlier)
        theirs = [[moves[i](v) for v in send] for i, send in zip(active, sends)]
        swapped = None if beside is None else jax.tree.map(swap_row, beside)
        self.arrived = (theirs, swapped)
        following = [None, None, None]
        for i, there in zip(active, theirs):
            kept = [picked(v, bits[i], axes[i]) for v in self.stages[i]]
            total = [k.astype(F32) + t.astype(F32) for k, t in zip(kept, there)]
            if i == 2:
                self.totals.append(total)
                continue
            total = [v.astype(k.dtype) for v, k in zip(total, kept)]
            if i == 0:
                total = [v.reshape((2, 2) + v.shape[1:]) for v in total]
            following[i + 1] = total
        self.stages = following
        return swapped

    def finish(self):
        while any(stage is not None for stage in self.stages):
            self.tick()


def attend_kernel(q_ref, k_ref, v_ref, o_ref):
    factor = 1.0 / math.sqrt(HEAD_DIM)
    for head in range(q_ref.shape[1] // HEAD_DIM):
        part = slice(head * HEAD_DIM, (head + 1) * HEAD_DIM)
        scores = right_product(q_ref[:, part], k_ref[:, part]) * factor
        raised = jnp.exp(scores - jnp.max(scores, axis=1, keepdims=True))
        chances = raised * (1.0 / jnp.sum(raised, axis=1, keepdims=True))
        o_ref[:, part] = matmul(chances.astype(BF), v_ref[:, part]).astype(BF)


def attend(qkv):
    rows, width = qkv.shape
    width //= 3
    block = 2 * HEAD_DIM
    steps = width // block
    return pl.pallas_call(
        attend_kernel,
        grid=(steps,),
        in_specs=[
            pl.BlockSpec((rows, block), lambda i: (0, i)),
            pl.BlockSpec((rows, block), lambda i: (0, steps + i)),
            pl.BlockSpec((rows, block), lambda i: (0, 2 * steps + i)),
        ],
        out_specs=pl.BlockSpec((rows, block), lambda i: (0, i)),
        out_shape=jax.ShapeDtypeStruct((rows, width), BF),
        compiler_params=pltpu.CompilerParams(vmem_limit_bytes=VMEM_BYTES),
        cost_estimate=lasting(6.0),
        name="attend",
    )(qkv, qkv, qkv)


def attend_back_kernel(q_ref, k_ref, v_ref, eo_ref, eq_ref, ek_ref, ev_ref):
    factor = 1.0 / math.sqrt(HEAD_DIM)
    for head in range(q_ref.shape[1] // HEAD_DIM):
        part = slice(head * HEAD_DIM, (head + 1) * HEAD_DIM)
        queries, keys, eo = q_ref[:, part], k_ref[:, part], eo_ref[:, part]
        scores = right_product(keys, queries) * factor
        raised = jnp.exp(scores - jnp.max(scores, axis=0, keepdims=True))
        chances = raised * (1.0 / jnp.sum(raised, axis=0, keepdims=True))
        ep = right_product(v_ref[:, part], eo)
        ev_ref[:, part] = matmul(chances.astype(BF), eo).astype(BF)
        inner = jnp.sum(ep * chances, axis=0, keepdims=True)
        es = (chances * (ep - inner)).astype(BF)
        ek_ref[:, part] = (matmul(es, queries) * factor).astype(BF)
        eq_ref[:, part] = (left_product(keys, es) * factor).T.astype(BF)


def attend_back(qkv, eo):
    rows, width = eo.shape
    block = 2 * HEAD_DIM
    steps = width // block
    return pl.pallas_call(
        attend_back_kernel,
        grid=(steps,),
        in_specs=[
            pl.BlockSpec((rows, block), lambda i: (0, i)),
            pl.BlockSpec((rows, block), lambda i: (0, steps + i)),
            pl.BlockSpec((rows, block), lambda i: (0, 2 * steps + i)),
            pl.BlockSpec((rows, block), lambda i: (0, i)),
        ],
        out_specs=[pl.BlockSpec((rows, block), lambda i: (0, i))] * 3,
        out_shape=[jax.ShapeDtypeStruct((rows, width), BF)] * 3,
        compiler_params=pltpu.CompilerParams(vmem_limit_bytes=VMEM_BYTES),
        cost_estimate=lasting(8.2),
        name="attend_back",
    )(qkv, qkv, qkv, eo)


def norm_parts(values):
    centred = values - jnp.mean(values, axis=-1, keepdims=True)
    spread = jnp.mean(centred * centred, axis=-1, keepdims=True)
    rate = lax.rsqrt(spread + epsilon)
    return centred * rate, rate


def pack_kernel(where_ref, *refs):
    *squares, up_ref, down_ref, branch_ref, wide_ref = refs
    side, core = where_ref[2], where_ref[3]
    shard, features = squares[0].shape[1:]
    half, part = features // 2, shard // 2
    unit_half = down_ref.shape[1] // 2
    columns = pl.ds(pl.multiple_of(core * half, 128), half)
    for position, square in enumerate(squares):
        branch_ref[:, position * half : (position + 1) * half] = square[0, :, columns]
    rows = up_ref[0, pl.ds(pl.multiple_of(side * part, 16), part), :]
    chosen = []
    for owner in range(up_ref.shape[2] // (2 * unit_half)):
        first = 2 * owner * unit_half
        low = rows[:, first : first + unit_half]
        high = rows[:, first + unit_half : first + 2 * unit_half]
        chosen.append(jnp.where(core == 0, low, high))
    wide_ref[:part, :] = jnp.concatenate(chosen, 1)
    for pair in range(2):
        first = pl.multiple_of(core * unit_half + side * shard, 16) + pair * part
        wide_ref[part:, pair * features : (pair + 1) * features] = down_ref[
            0, pl.ds(first, part), :
        ]


def pack(where, squares, up, down, layer):
    members = (*squares, up, down)
    shard, features = squares[0].shape[1:]
    shape = (shard, 2 * features)
    return pl.pallas_call(
        pack_kernel,
        grid=(1,),
        in_specs=[pl.BlockSpec(memory_space=pltpu.SMEM)]
        + [pl.BlockSpec((1,) + v.shape[1:], lambda i: (layer, 0, 0)) for v in members],
        out_specs=[pl.BlockSpec(shape, lambda i: (0, 0))] * 2,
        out_shape=[jax.ShapeDtypeStruct(shape, BF)] * 2,
        compiler_params=pltpu.CompilerParams(vmem_limit_bytes=60 * 1024 * 1024),
        cost_estimate=lasting(3.0),
        name="pack",
    )(where, *members)


def norm_next_kernel(base_ref, partial_ref, *refs):
    *theirs, bias_ref, scale_ref, shift_ref, value_ref, normed_ref = refs
    value = base_ref[...] + partial_ref[...] + bias_ref[...]
    for there in theirs:
        value = value + there[...].astype(F32)
    value_ref[...] = value
    flat, _ = norm_parts(value)
    normed_ref[...] = (flat * scale_ref[...] + shift_ref[...]).astype(BF)


def norm_next(base, parts, bias, scale, shift):
    rows, features = base.shape
    block = pl.BlockSpec((rows // 4, features), lambda i: (i, 0))
    line = pl.BlockSpec((1, features), lambda i: (0, 0))
    return pl.pallas_call(
        norm_next_kernel,
        grid=(4,),
        in_specs=[block] * (1 + len(parts)) + [line] * 3,
        out_specs=[block] * 2,
        out_shape=[
            jax.ShapeDtypeStruct((rows, features), F32),
            jax.ShapeDtypeStruct((rows, features), BF),
        ],
        compiler_params=pltpu.CompilerParams(vmem_limit_bytes=VMEM_BYTES),
        cost_estimate=lasting(2.9),
        name="norm_next",
    )(base, *parts, *(v.reshape(1, features) for v in (bias, scale, shift)))


def norm_back_kernel(offset_ref, partial_ref, there_ref, value_ref, scale_ref, base_ref, *outs):
    out_ref, low_ref, sums_ref = outs

    @pl.when(pl.program_id(0) == 0)
    def _():
        sums_ref[...] = jnp.zeros_like(sums_ref)

    grad = partial_ref[...] + there_ref[...].astype(F32)
    flat, rate = norm_parts(value_ref[...])
    inner = grad * scale_ref[...]
    mean_inner = jnp.mean(inner, axis=-1, keepdims=True)
    mean_cross = jnp.mean(inner * flat, axis=-1, keepdims=True)
    total = base_ref[...] + rate * (inner - mean_inner - flat * mean_cross)
    out_ref[...] = total
    low = total.astype(BF)
    low_ref[...] = low
    sums_ref[0:1] += jnp.sum(grad * flat, axis=0, keepdims=True)
    sums_ref[1:2] += jnp.sum(grad, axis=0, keepdims=True)
    sums_ref[2:3] += jnp.sum(low.astype(F32), axis=0, keepdims=True)


def norm_back(partial, there, value, scale, base, offset):
    rows, features = there.shape
    block = rows // 4
    steps = rows // block
    moved = pl.BlockSpec((block, features), lambda i, w: (w[0] * steps + i, 0))
    plain = pl.BlockSpec((block, features), lambda i, w: (i, 0))
    return pl.pallas_call(
        norm_back_kernel,
        grid_spec=pltpu.PrefetchScalarGridSpec(
            num_scalar_prefetch=1,
            grid=(steps,),
            in_specs=[
                moved,
                plain,
                moved,
                pl.BlockSpec((1, features), lambda i, w: (0, 0)),
                moved,
            ],
            out_specs=[plain, plain, pl.BlockSpec((8, features), lambda i, w: (0, 0))],
        ),
        out_shape=[
            jax.ShapeDtypeStruct((rows, features), F32),
            jax.ShapeDtypeStruct((rows, features), BF),
            jax.ShapeDtypeStruct((8, features), F32),
        ],
        compiler_params=pltpu.CompilerParams(vmem_limit_bytes=VMEM_BYTES),
        cost_estimate=lasting(3.8),
        name="norm_back",
    )(offset, partial, there, value, scale.reshape(1, features), base)


def gelu_parts(values):
    below = 0.5 * (1.0 + lax.erf(values * math.sqrt(0.5)))
    density = jnp.exp(-0.5 * values * values) * (1.0 / math.sqrt(2.0 * math.pi))
    return values * below, below + values * density


def settle_kernel(where_ref, *refs):
    *squares, up, down = refs[-6:]
    side, core = where_ref[2], where_ref[3]
    shard, features = squares[0].shape[1:]
    half, part = features // 2, shard // 2
    unit_half = down.shape[1] // 2
    owners = up.shape[2] // (2 * unit_half)
    pieces = 3 if refs[1].shape[0] == shard else 2
    mine_ref, *mine_wide = refs[:pieces]
    other_ref, *other_wide = refs[pieces : 2 * pieces]
    here = pl.ds(pl.multiple_of(core * half, 128), half)
    there = pl.ds(pl.multiple_of((1 - core) * half, 128), half)
    for position, target in enumerate(squares):
        columns = slice(position * half, (position + 1) * half)
        target[0, :, here] = mine_ref[:, columns].astype(F32)
        target[0, :, there] = other_ref[:, columns].astype(F32)
    spread = [0] if pieces == 2 else [side, 1 - side]
    rows = shard if pieces == 2 else part
    for where, mine_part, other_part in zip(spread, mine_wide, other_wide):
        mine, other = mine_part[:rows].astype(F32), other_part[:rows].astype(F32)
        low = jnp.where(core == 0, mine, other)
        high = jnp.where(core == 0, other, mine)
        target = pl.ds(where * rows if pieces == 2 else pl.multiple_of(where * rows, 8), rows)
        for owner in range(owners):
            columns = slice(owner * unit_half, (owner + 1) * unit_half)
            up[0, target, 2 * owner * unit_half : 2 * (owner + 1) * unit_half] = jnp.concatenate(
                [low[:, columns], high[:, columns]], 1
            )
        for pair in range(2):
            columns = slice(pair * features, (pair + 1) * features)
            for source, place_core in ((mine_part, core), (other_part, 1 - core)):
                first = place_core * unit_half + where * shard
                target = pl.ds(pl.multiple_of(first, 8) + pair * rows, rows)
                down[0, target] = source[rows:, columns].astype(F32)


def settle(core, pieces, earlier, layer, shapes):
    size = sum(math.prod(shape[1:]) for shape in shapes)
    return pl.pallas_call(
        settle_kernel,
        grid=(1,),
        in_specs=[pl.BlockSpec(memory_space=pltpu.SMEM)]
        + [pl.BlockSpec(piece.shape, lambda i: (0, 0)) for piece in pieces]
        + [pl.BlockSpec(memory_space=pl.ANY)] * len(earlier),
        out_specs=[
            pl.BlockSpec((1,) + shape[1:], lambda i: (layer, 0, 0)) for shape in shapes
        ],
        out_shape=[jax.ShapeDtypeStruct(shape, F32) for shape in shapes],
        input_output_aliases={1 + len(pieces) + i: i for i in range(len(earlier))},
        compiler_params=pltpu.CompilerParams(vmem_limit_bytes=VMEM_BYTES),
        cost_estimate=lasting(2.0),
        name="settle",
    )(core, *pieces, *earlier)


def per_device(
    activations,
    upstream,
    first_scale,
    first_shift,
    query_weight,
    query_bias,
    key_weight,
    value_weight,
    value_bias,
    output_weight,
    output_bias,
    second_scale,
    second_shift,
    up_weight,
    up_bias,
    down_weight,
    down_bias,
):
    owners = lax.axis_size("wt")
    seat = lax.axis_index("seq")
    core, side = seat % 2, seat // 2
    frames_here, features = activations.shape[1:]
    half = features // 2
    shard = features // owners
    units = up_weight.shape[2]
    unit_shard = units // owners
    unit_half = unit_shard // 2

    def to_chip(values):
        kept = lax.dynamic_index_in_dim(values, side, 0, keepdims=False)
        sent = lax.dynamic_index_in_dim(values, 1 - side, 0, keepdims=False)
        mine = jnp.concatenate([kept, swap_row(sent)], 0)
        return by_core(core, mine, swap_core(mine), 0)

    def from_chip(mine, other):
        kept = mine[:frames_here]
        return jnp.where(side == 0, jnp.stack([kept, other]), jnp.stack([other, kept]))

    def by_side(mine, there):
        low, high = jnp.where(side == 0, mine, there), jnp.where(side == 0, there, mine)
        part = shard // 2
        low_down, high_down = low[part:], high[part:]
        return jnp.concatenate(
            [
                low[:part],
                high[:part],
                jnp.concatenate([low_down[:, :features], high_down[:, :features]], 1),
                jnp.concatenate([low_down[:, features:], high_down[:, features:]], 1),
            ],
            0,
        )

    def own_rows(values):
        return lax.dynamic_slice_in_dim(values, core * 2 * frames_here, 2 * frames_here, 0)

    def half_columns(values):
        return lax.dynamic_slice_in_dim(values, core * half, half, 1)

    direct = owners == 8
    own = lax.axis_index("wt")
    line, across = own // 2, own % 2
    where = jnp.stack([line, across, side, core]).astype(jnp.int32)

    down_in = to_chip(upstream)
    shards = {}
    for layer in range(LAYERS):
        shards["branch", layer] = jnp.concatenate(
            [
                half_columns(query_weight[layer]),
                half_columns(key_weight[layer]),
                half_columns(value_weight[layer]),
                half_columns(output_weight[layer]),
            ],
            1,
        )
    for layer in range(LAYERS):
        shards["up", layer] = picked(
            up_weight[layer].reshape(shard, owners, 2, unit_half), core, 2
        ).reshape(shard, units // 2)
        shards["down", layer] = lax.dynamic_slice_in_dim(
            down_weight[layer], core * unit_half, unit_half, 0
        )
    members = dict(
        first_scale=first_scale,
        first_shift=first_shift,
        query_bias=query_bias,
        value_bias=value_bias,
        output_bias=output_bias,
        second_scale=second_scale,
        second_shift=second_shift,
        down_bias=down_bias,
    )
    narrow = len(VECTORS) * shard
    packed = jnp.concatenate([members[name] for name in VECTORS] + [up_bias], 1)
    gathered = {}
    if direct:

        squares = (query_weight, key_weight, value_weight, output_weight)
        branch_piece, wide_piece = zip(
            *(pack(where, squares, up_weight, down_weight, layer) for layer in range(LAYERS))
        )

        wide, branch = [None, None], [None, None]
        wide_far, branch_far = [None, None], [None, None]
        wide_there, wide_far_there = [None, None], [None, None]
        wide_hop, first = doubled(wide_piece[0][None], 2)

        wide[0], tied = doubled(after(wide_hop, first), 1)
        branch_hop, also = doubled(after(branch_piece[0][None], first), 2)
        packed_hop, _ = doubled(after(packed[None], first), 2)
        earlier = (tied, also, down_in)

        wide_far[0] = swap_pair(after(wide[0], earlier))
        wide_there[0] = swap_row(after(wide[0], earlier))
        branch[0], tied = doubled(after(branch_hop, earlier), 1)
        wide_hop, also = doubled(after(wide_piece[1][None], earlier), 2)
        packed_line, _ = doubled(after(packed_hop, earlier), 1)
        earlier = (tied, also, wide_far[0], wide_there[0])

        branch_far[0] = swap_pair(after(branch[0], earlier))
        wide_far_there[0] = swap_row(after(wide_far[0], earlier))
        wide[1], tied = doubled(after(wide_hop, earlier), 1)
        branch_hop, also = doubled(after(branch_piece[1][None], earlier), 2)
        packed_far = swap_pair(after(packed_line, earlier))
        earlier = (tied, also, branch_far[0], wide_far_there[0])

        wide_far[1] = swap_pair(after(wide[1], earlier))
        wide_there[1] = swap_row(after(wide[1], earlier))
        branch[1], tied = doubled(after(branch_hop, earlier), 1)
        third = (wide_far[1], wide_there[1], tied)

        branch_far[1], wide_far_there[1] = lax.optimization_barrier(
            (swap_pair(after(branch[1], third)), swap_row(after(wide_far[1], third)))
        )

        for layer in range(LAYERS):
            pieces = (branch[layer], branch_far[layer])
            (gathered["in", layer],) = place(
                fill_in,
                where,
                tuple((v, 3 * half, 0) for v in pieces),
                ((2, shard, 3 * half),),
                "place_in",
            )
            gathered["in", layer] = gathered["in", layer].reshape(features, 3 * half)
            swapped = swap_core(jnp.concatenate([v[:, :, 3 * half :] for v in pieces], 2))
            (gathered["out", layer],) = place(
                fill_out,
                where,
                tuple((v, half, 3) for v in pieces) + ((swapped, half, 0), (swapped, half, 1)),
                ((2, shard, features),),
                "place_out",
            )
            gathered["out", layer] = gathered["out", layer].reshape(features, features)
            width = 2 * features
            pieces = (wide[layer], wide_far[layer], wide_there[layer])
            placed = place(
                fill_wide,
                where,
                tuple((v, width, 0) for v in pieces),
                ((2, 2, shard // 2, width), (2, 2, 2, shard // 2, features)),
                "place_wide",
            )
            gathered["up", layer], gathered["down", layer] = place_last(
                where, wide_far_there[layer], placed
            )
            gathered["up", layer] = gathered["up", layer].reshape(features, units // 2)
            gathered["down", layer] = gathered["down", layer].reshape(units // 2, features)
    else:
        for layer in range(LAYERS):
            for kind in ("up", "down"):
                gathered[kind, layer] = lax.all_gather(
                    shards[kind, layer], "wt", axis=0, tiled=True
                )
            branch = lax.all_gather(shards["branch", layer], "wt", axis=0, tiled=True)
            gathered["in", layer] = branch[:, : 3 * half]
            out_half = branch[:, 3 * half :]
            gathered["out", layer] = by_core(core, out_half, swap_core(out_half), 1)
    if direct:
        spread = jnp.stack([packed_line, packed_far], 1)
        spread = spread.reshape((2, 2, 2) + packed.shape).swapaxes(0, 1)
        spread = spread.reshape((owners // 2, 2) + packed.shape)
        for bit in LINE_STEPS:
            turned = spread.reshape((owners // (4 * bit), 2, bit, 2) + packed.shape)
            spread = jnp.where((line & bit) == 0, turned, turned[:, ::-1]).reshape(spread.shape)
        spread = jnp.where(across == 0, spread, spread[:, ::-1]).reshape(
            (owners,) + packed.shape
        )
    else:
        spread = lax.all_gather(packed, "wt", axis=0, tiled=False)
    vector_rows = (
        spread[:, :, :narrow]
        .reshape(owners, LAYERS * len(VECTORS), shard)
        .swapaxes(0, 1)
        .reshape(LAYERS * len(VECTORS), features)
        .astype(F32)
    )
    vectors = [
        {
            name: vector_rows[layer * len(VECTORS) + position]
            for position, name in enumerate(VECTORS)
        }
        for layer in range(LAYERS)
    ]
    unit_rows = (
        picked(spread[:, :, narrow:].reshape(owners, LAYERS, 2, unit_half), core, 2)
        .swapaxes(0, 1)
        .reshape(LAYERS, units // 2)
        .astype(F32)
    )

    weights = [
        tuple(gathered[kind, layer] for kind in ("in", "out", "up", "down"))
        for layer in range(LAYERS)
    ]

    hidden = to_chip(activations).astype(F32)
    kept = []
    for layer in range(LAYERS):
        vec = vectors[layer]
        in_weight, out_weight, up, down = weights[layer]
        if layer == 0:
            flat, _ = norm_parts(hidden)
            normed = (flat * vec["first_scale"] + vec["first_shift"]).astype(BF)
        in_bias = jnp.concatenate(
            [
                lax.dynamic_slice_in_dim(vec["query_bias"], core * half, half, 0),
                jnp.zeros((half,), F32),
                lax.dynamic_slice_in_dim(vec["value_bias"], core * half, half, 0),
            ]
        )
        qkv = (matmul(normed, in_weight) + in_bias).astype(BF)
        mixture_half = attend(qkv)
        mixture = by_core(core, mixture_half, swap_core(mixture_half), 1)
        middle, second = norm_next(
            hidden,
            (matmul(mixture, out_weight),),
            vec["output_bias"],
            vec["second_scale"],
            vec["second_shift"],
        )
        if direct and layer == 0:
            second = after(second, third)
        upward = matmul(second, up) + unit_rows[layer]
        activated, slope = gelu_parts(upward)
        activated = activated.astype(BF)
        slope = slope.astype(BF)
        kept.append((hidden, normed, qkv, mixture, middle, second, activated, slope))
        partial = matmul(activated, down)
        if layer + 1 < LAYERS:
            hidden, normed = norm_next(
                middle,
                (partial, swap_core(partial.astype(BF))),
                vec["down_bias"],
                vectors[layer + 1]["first_scale"],
                vectors[layer + 1]["first_shift"],
            )
        else:
            last_rows = (partial, middle)

    grad_hidden = down_in.astype(F32)
    grad_down_bias = column_sums(down_in)[None]
    vector_grads = [None] * LAYERS
    settled = ()
    reducer = Reducer()
    row_core = core.reshape(1).astype(jnp.int32)
    no_offset = jnp.zeros((1,), jnp.int32)
    matrix_shapes = tuple(
        (LAYERS,) + shape
        for shape in ((shard, features),) * 4 + ((shard, units), (unit_shard, features))
    )
    for layer in reversed(range(LAYERS)):
        vec = vectors[layer]
        in_weight, out_weight, up, down = weights[layer]
        hidden, normed, qkv, mixture, middle, second, activated, slope = kept[layer]
        grad_down = left_product(activated, down_in).astype(BF)
        grad_upward = (slope.astype(F32) * right_product(down_in, down)).astype(BF)
        grad_up = left_product(second, grad_upward).astype(BF)
        if layer > 0:
            grad_up = grad_up.reshape(owners, shard, units // 2)
            reducer.tick([grad_down.reshape(owners, unit_half, features)])
        else:
            grad_up = grad_up.reshape(owners, 2, shard // 2, units // 2)
            grad_down = grad_down.reshape(owners, 2, 2, shard // 2, features)
            grad_down = jnp.concatenate([grad_down[:, :, 0], grad_down[:, :, 1]], -1)
            down_there = reducer.tick([grad_branch], beside=picked(grad_down, 1 - side, 1))
        grad_up_bias = column_sums(grad_upward)
        partial = right_product(grad_upward, up)
        there = swap_core(partial.astype(BF))
        grad_middle, branch_in, second_sums = norm_back(
            partial, there, middle, vec["second_scale"], grad_hidden, no_offset
        )
        grad_out = left_product(mixture, half_columns(branch_in))
        out_rows = lax.dynamic_slice_in_dim(out_weight, core * half, half, 0)
        grad_mixture = right_product(branch_in, out_rows).astype(BF)
        grad_qkv = jnp.concatenate(attend_back(qkv, grad_mixture), 1)
        grad_in = left_product(normed, grad_qkv).astype(BF)
        grad_branch = jnp.concatenate([grad_in, grad_out.astype(BF)], 1)
        grad_branch = grad_branch.reshape(owners, shard, 2 * features)
        if layer > 0:
            reducer.tick([grad_up], grad_branch)
        else:
            last_rows = after(last_rows, reducer.arrived) if direct else last_rows
            up_there = reducer.tick([grad_branch], beside=picked(grad_up, 1 - side, 1))
            grad_wide = jnp.concatenate(
                [
                    (picked(grad_up, side, 1).astype(F32) + up_there.astype(F32)).astype(BF),
                    (picked(grad_down, side, 1).astype(F32) + down_there.astype(F32)).astype(BF),
                ],
                1,
            )
        grad_in_bias = column_sums(grad_qkv)
        partial = right_product(grad_qkv, in_weight)
        below = grad_down_bias
        if layer > 0:
            there = swap_core(partial.astype(BF))
            grad_hidden, down_in, first_sums = norm_back(
                partial, there, hidden, vec["first_scale"], grad_middle, no_offset
            )
            grad_down_bias = first_sums[2:3]
        else:
            theirs = lax.dynamic_slice_in_dim(
                partial, (1 - core) * 2 * frames_here, 2 * frames_here, 0
            )
            there = swap_core(theirs.astype(BF))
            before, _, first_sums = norm_back(
                partial, there, hidden, vec["first_scale"], grad_middle, row_core
            )

        twice = jnp.stack([grad_in_bias[:half], grad_in_bias[2 * half :]])
        rows = jnp.concatenate(
            [
                first_sums[:2],
                jnp.concatenate([twice, twice], 1),
                second_sums[2:3],
                second_sums[:2],
                below,
            ],
            0,
        )
        place_row = lax.broadcasted_iota(jnp.int32, rows.shape, 0)
        on_right = lax.broadcasted_iota(jnp.int32, rows.shape, 1) >= half
        counted = jnp.where((place_row == 2) | (place_row == 3), on_right == (core == 1), core == 0)
        if layer == 0:
            counted = counted | (place_row < 2)
        vector_grads[layer] = (jnp.where(counted, rows, 0.0), grad_up_bias)

    packed = jnp.stack([rows for rows, _ in vector_grads])
    packed = packed.reshape(LAYERS * len(VECTORS), owners, shard).swapaxes(0, 1)
    packed = packed.reshape(owners, LAYERS * narrow)
    from_units = jnp.stack([values for _, values in vector_grads])
    from_units = from_units.reshape(LAYERS, owners, unit_half).swapaxes(0, 1)
    from_units = from_units.reshape(owners, LAYERS * unit_half)
    packed = jnp.concatenate([packed, from_units], 1)
    partial, middle = last_rows
    theirs = lax.dynamic_slice_in_dim(
        partial, (1 - core) * 2 * frames_here, 2 * frames_here, 0
    )
    total = own_rows(partial) + swap_core(theirs.astype(BF))
    last_bias = vectors[LAYERS - 1]["down_bias"]
    result_rows = (own_rows(middle) + last_bias + total).astype(BF)
    chip_there = reducer.tick(
        [grad_wide, packed], beside=(result_rows[frames_here:], before[frames_here:])
    )
    reducer.finish()
    result = from_chip(result_rows, chip_there[0])
    input_grad = from_chip(before, chip_there[1])
    for layer in reversed(range(LAYERS)):
        if layer > 0:
            (grad_down,), (grad_up,), (grad_branch,) = reducer.totals[:3]
            grad_wide = jnp.concatenate(
                [grad_up, jnp.concatenate([grad_down[:shard], grad_down[shard:]], 1)], 0
            )
        else:
            (grad_branch,), (grad_wide, packed) = reducer.totals[3:]

        def over_sides(values):
            values = values.astype(BF)
            there = swap_row(values)
            if layer > 0:
                there = after(there, reducer.arrived)
            values = (values.astype(F32) + there.astype(F32)).astype(BF)
            return values, swap_core(values)

        if layer > 0:
            mine, other = over_sides(jnp.concatenate([grad_branch, grad_wide], 0))
            mine, other = (mine[:shard], mine[shard:]), (other[:shard], other[shard:])
        else:
            mine, other = over_sides(grad_branch)
            wide_mine = grad_wide.astype(BF)
            wide_there = after(swap_row(wide_mine), settled)
            mine = (mine, wide_mine, wide_there)
            other = (other, swap_core(wide_mine), swap_core(wide_there))
        if direct:
            settled = settle(where, mine + other, settled, layer, matrix_shapes)
            continue
        if layer == 0:
            mine, other = (mine[0], by_side(*mine[1:])), (other[0], by_side(*other[1:]))
        low = [jnp.where(core == 0, m, o).astype(F32) for m, o in zip(mine, other)]
        high = [jnp.where(core == 0, o, m).astype(F32) for m, o in zip(mine, other)]
        done = []
        for position in range(4):
            part = slice(position * half, (position + 1) * half)
            done.append(jnp.concatenate([low[0][:, part], high[0][:, part]], 1))

        def up_part(values):
            return values[:shard].reshape(shard, owners, unit_half)

        def down_part(values):
            return jnp.concatenate([values[shard:, :features], values[shard:, features:]], 0)

        done.append(jnp.stack([up_part(low[1]), up_part(high[1])], 2).reshape(shard, units))
        done.append(jnp.concatenate([down_part(low[1]), down_part(high[1])], 0))
        if not settled:
            settled = tuple(jnp.zeros(shape, F32) for shape in matrix_shapes)
        settled = tuple(total.at[layer].set(part) for total, part in zip(settled, done))

    packed = packed + swap_row(packed)
    other = swap_core(packed)
    narrow_sum = (packed + other)[: LAYERS * narrow].reshape(LAYERS, len(VECTORS), shard)
    unit_mine = packed[LAYERS * narrow :].reshape(LAYERS, unit_half)
    unit_other = other[LAYERS * narrow :].reshape(LAYERS, unit_half)
    summed = {name: narrow_sum[:, position] for position, name in enumerate(VECTORS)}
    summed["up_bias"] = by_core(core, unit_mine, unit_other, 1)

    query, key, value, output, up, down = settled
    final = (
        summed["first_scale"],
        summed["first_shift"],
        query,
        summed["query_bias"],
        key,
        value,
        summed["value_bias"],
        output,
        summed["output_bias"],
        summed["second_scale"],
        summed["second_shift"],
        up,
        summed["up_bias"],
        down,
        summed["down_bias"],
    )
    return (result, input_grad) + final


def solution(mesh):
    rows, vector, matrix = P("wt", "seq", None), P(None, "wt"), P(None, "wt", None)
    parameters = (
        vector,
        vector,
        matrix,
        vector,
        matrix,
        matrix,
        vector,
        matrix,
        vector,
        vector,
        vector,
        matrix,
        vector,
        matrix,
        vector,
    )
    specs = (rows, rows) + parameters
    return jax.shard_map(
        per_device, mesh=mesh, in_specs=specs, out_specs=specs, check_vma=False
    )
```
